32 devices in a mesh: tm: 8 (over z, y), head: 4 (over x, core).
Axes of the slice: x: 2, y: 2, z: 4, core: 2. Of those that a mesh axis runs over, the one named last changes fastest.
Arguments:
- queries: bfloat16 [8, 384, 24, 128], P('tm', None, 'head'), may hold values from -40 to 40
- key_vectors: bfloat16 [8, 384, 24, 128], P('tm', None, 'head'), may hold values from -40 to 40
- value_vectors: bfloat16 [8, 384, 24, 128], P('tm', None, 'head'), may hold values from -6 to 6
- head_class: int32 [24], replicated, may hold values from 0 to 1, as said below
- frame_mask: int32 [4, 4], replicated, may hold values from 0 to 1, as said below
Outputs:
- attended: bfloat16 [8, 384, 24, 128], P('tm', None, 'head')
The draws below stay inside these ranges and needn't reach their ends.
Inputs may be any that keep to these rules, and one draw needn't show every extreme that they name: `head_class`: head group g holds heads g * 6 to g * 6 + 5; each group holds 1 or 5 temporal heads, and groups 2k and 2k + 1 hold 6 temporal heads together. `frame_mask`: the diagonal is all ones.
All inputs are finite; a program needn't handle non-finite values.
Results may differ from the reference program's by a relative error of at most 0.0042.
Values may be sent and summed in bfloat16 or wider, within the bound.
No kernel may reach another device: no remote copies, remote signals or barrier semaphores. Data moves between devices by JAX's collectives and lax.ppermute only.
A program may use at most 64 MiB of HBM per device.

```python
import jax
import jax.numpy as jnp
from jax import lax

HEADS = 24
HD = 128
PATCHES = 384
FB = 4
FRAMES = 8
HG = 6
LEAST_T = 1
MOST_T = 5
FBLK = 2


def shared_parts(key):
    shape = (FRAMES, PATCHES, HEADS, HD)
    base = jax.random.normal(key, shape, jnp.float32)
    patch_id = lax.broadcasted_iota(jnp.int32, shape, 1)
    head_id = lax.broadcasted_iota(jnp.int32, shape, 2)
    strength = 3.2 + 1.5 * ((patch_id // 16 + head_id) % 3).astype(jnp.float32)
    return base * strength


def draw_queries(key, part):
    aligned = shared_parts(key)
    key = jax.random.fold_in(key, 7)
    return jax.random.normal(key, aligned.shape, jnp.float32).astype(jnp.bfloat16)


def draw_key_vectors(key, part):
    aligned = shared_parts(key)
    key = jax.random.fold_in(key, 11)
    return jax.random.normal(key, aligned.shape, jnp.float32).astype(jnp.bfloat16)


def draw_head_class(key, part):
    key = jax.random.fold_in(key, 5)
    first_key, second_key = jax.random.split(key)
    pair_count = HEADS // HG // 2
    flipped = jax.random.randint(first_key, (pair_count,), 0, 2)
    is_heavy = jnp.stack([flipped, 1 - flipped], axis=1).reshape(-1)
    group_count = LEAST_T + is_heavy * (MOST_T - LEAST_T)
    ranking = jax.vmap(lambda one_key: jax.random.permutation(one_key, HG))(jax.random.split(second_key, 2 * pair_count))
    return (ranking < group_count[:, None]).astype(jnp.int32).reshape(-1)


def draw_frame_mask(key, part):
    key = jax.random.fold_in(key, 3)
    random_bits = jax.random.randint(key, (FB, FB), 0, 2)
    return jnp.maximum(random_bits, jnp.eye(FB, dtype=jnp.int32)).astype(jnp.int32)


def block_levels(key, shape, cuts, low, largest):
    loudness = 1.0
    for position, parts in cuts:
        draws = jax.random.uniform(jax.random.fold_in(jax.random.fold_in(key, 6), position), (parts,), jnp.float32, low / len(cuts), largest / len(cuts))
        loudness = loudness * jnp.repeat(jnp.exp(draws), shape[position] // parts).reshape((-1,) + (1,) * (len(shape) - 1 - position))
    return loudness


def noise(own_key, extent, scale, most, pieces=(), held_as=jnp.bfloat16):
    values = jax.random.normal(own_key, extent, jnp.float32) * scale
    if len(pieces) > 0:
        values = block_levels(own_key, extent, pieces, -0.22, 0.18) * values
    return jnp.clip(values, min=-most, max=most).astype(held_as)


def setup_inputs(seed: int = 0) -> dict:
    arg_keys = jax.random.split(jax.random.key(seed), 6)
    return {
        "queries": draw_queries(jax.random.fold_in(arg_keys[5], 71), 0),
        "key_vectors": draw_key_vectors(jax.random.fold_in(arg_keys[5], 71), 0),
        "value_vectors": noise(arg_keys[2], (FRAMES, PATCHES, HEADS, HD), 1.0, 6.0, ((0, 8), (2, 4))),
        "head_class": draw_head_class(jax.random.fold_in(arg_keys[5], 71), 0),
        "frame_mask": draw_frame_mask(jax.random.fold_in(arg_keys[5], 71), 0),
    }


def reference(queries, key_vectors, value_vectors, head_class, frame_mask):
    score_scale = HD ** -0.5
    sorted_heads = jnp.argsort(head_class, stable=True).astype(jnp.int32)
    head_rank = jnp.argsort(sorted_heads).astype(jnp.int32)
    half_heads = HEADS // 2
    spatial_heads = sorted_heads[:half_heads]
    temporal_heads = sorted_heads[half_heads:]

    def spatial_frame(triple):
        query_block, key_block, value_block = triple
        scores = jnp.einsum('ihd,jhd->hij', query_block.astype(jnp.float32), key_block.astype(jnp.float32)) * score_scale
        peak = jnp.max(scores, axis=-1, keepdims=True)
        exponent = jnp.exp(scores - peak)
        totals = jnp.sum(exponent, axis=-1)
        weights = lax.optimization_barrier(exponent.astype(jnp.bfloat16)).astype(jnp.float32)
        blended = jnp.einsum('hij,jhd->ihd', weights, value_block.astype(jnp.float32))
        return (blended / jnp.transpose(totals)[:, :, None]).astype(jnp.bfloat16)

    spatial_in = tuple(jnp.take(a, spatial_heads, axis=2) for a in (queries, key_vectors, value_vectors))
    spatial = lax.map(spatial_frame, spatial_in)

    frame_block = jnp.arange(FRAMES, dtype=jnp.int32) // FBLK
    allowed = frame_mask[frame_block][:, frame_block] == 1

    def temporal_position(triple):
        query_block, key_block, value_block = triple
        scores = jnp.einsum('fhd,ghd->hfg', query_block.astype(jnp.float32), key_block.astype(jnp.float32)) * score_scale
        scores = jnp.where(allowed[None], scores, jnp.float32(-1e30))
        peak = jnp.max(scores, axis=-1, keepdims=True)
        exponent = jnp.where(allowed[None], jnp.exp(scores - peak), jnp.float32(0.0))
        totals = jnp.sum(exponent, axis=-1)
        weights = lax.optimization_barrier(exponent.astype(jnp.bfloat16)).astype(jnp.float32)
        blended = jnp.einsum('hfg,ghd->fhd', weights, value_block.astype(jnp.float32))
        return (blended / jnp.transpose(totals)[:, :, None]).astype(jnp.bfloat16)

    temporal_in = tuple(jnp.swapaxes(jnp.take(a, temporal_heads, axis=2), 0, 1) for a in (queries, key_vectors, value_vectors))
    temporal = jnp.swapaxes(lax.map(temporal_position, temporal_in), 0, 1)
    combined = jnp.concatenate([spatial, temporal], axis=2)
    return jnp.take(combined, head_rank, axis=2)
```

```python
import functools
import math

import jax
import jax.numpy as jnp
from jax import lax
from jax.experimental import pallas as pl
from jax.experimental.pallas import tpu as pltpu
from jax.sharding import PartitionSpec as P

ROWS = 16
NEGATIVE = -1e30


def rank_heads(class_ref, order_ref, group_heads):
    base = lax.axis_index("head") * group_heads
    temporal = jnp.int32(0)
    for head in range(group_heads):
        is_temporal = class_ref[base + head]
        slot = jnp.where(is_temporal == 1, temporal, group_heads + head - temporal)
        order_ref[slot] = jnp.int32(head)
        temporal = temporal + is_temporal
    return temporal


def softmax_rows(scores):
    peak = jnp.max(scores, axis=-1, keepdims=True)
    exponent = jnp.exp(scores - peak)
    return exponent, jnp.sum(exponent, axis=-1, keepdims=True)


def attend(triples, bias=None):
    factor = triples[0][0].shape[-1] ** -0.5 * math.log2(math.e)
    scores = [
        lax.dot_general(query, key, (((1,), (1,)), ((), ())), preferred_element_type=jnp.float32)
        for query, key, _ in triples
    ]
    if bias is not None:
        scores = [score + bias for score in scores]
    peaks = [jnp.max(score, axis=-1, keepdims=True) for score in scores]
    exponents = [jnp.exp2((score - peak) * factor) for score, peak in zip(scores, peaks)]
    totals = [jnp.sum(exponent, axis=-1, keepdims=True) for exponent in exponents]
    blended = [
        jnp.dot(exponent.astype(jnp.bfloat16), value, preferred_element_type=jnp.float32)
        for exponent, (_, _, value) in zip(exponents, triples)
    ]
    return [(blend / total).astype(jnp.bfloat16) for blend, total in zip(blended, totals)]


def copy_all(copies, sems):
    started = [pltpu.make_async_copy(source, target, sems.at[i]) for i, (source, target) in enumerate(copies)]
    for copy in started:
        copy.start()

    def wait():
        for copy in started:
            copy.wait()

    return wait


def hand_kernel(sizes, class_ref, q_ref, k_ref, v_ref, out_ref, token_ref, order_ref, sems):
    group_heads, most, least = sizes
    handed = (most - least) // 2
    temporal = rank_heads(class_ref, order_ref, group_heads)
    first = jnp.where(temporal == most, most - handed, group_heads)
    copies = []
    for slot in range(handed):
        head = order_ref[first + slot]
        copies += [(ref.at[head], out_ref.at[slot, part]) for part, ref in enumerate((q_ref, k_ref, v_ref))]
    copy_all(copies, sems)()
    token_ref[...] = jnp.zeros_like(token_ref)


def load_kernel(q_ref, k_ref, v_ref, token_ref, q_out, k_out, v_out, sems):
    copies = [
        (ref.at[head], out.at[head])
        for ref, out in ((q_ref, q_out), (k_ref, k_out), (v_ref, v_out))
        for head in range(ref.shape[0])
    ]
    copy_all(copies, sems)()


def spatial_kernel(sizes, class_ref, mask_ref, q_ref, k_ref, v_ref, out_ref, bias_ref, order_ref):
    group_heads, ranks, blocks = sizes
    temporal = rank_heads(class_ref, order_ref, group_heads)

    def body(slot, carry):
        head = order_ref[group_heads + slot]
        (out_ref[head],) = attend([(q_ref[head], k_ref[head], v_ref[head])])
        return carry

    lax.fori_loop(0, group_heads - temporal, body, 0)
    fill_bias(bias_ref, mask_ref, frames_held(ranks), blocks)


def distances(ranks):
    far, near = list(range(ranks // 2, ranks)), list(range(1, ranks // 2))[::-1]
    return [0, *far[:1], *near[-2:-1], *far[1:2], *near[:-2], *near[-1:], *far[2:]]


def pack_kernel(sizes, class_ref, q_ref, k_ref, v_ref, given_ref, *rest):
    group_heads, most, least, ranks, share = sizes
    handed = (most - least) // 2
    out_refs, order_ref = rest[:ranks], rest[ranks]
    temporal = rank_heads(class_ref, order_ref, group_heads)
    me = lax.axis_index("tm")
    rows = [pl.ds(pl.multiple_of((me ^ step) * share, ROWS), share) for step in range(ranks)]

    def put(slot, sources):
        for part, source in enumerate(sources):
            for step in range(ranks):
                out_refs[step][slot, part] = source[rows[step], :]

    def own(slots):
        for slot in slots:
            head = order_ref[slot]
            put(slot, [ref.at[head] for ref in (q_ref, k_ref, v_ref)])

    own(range(least))

    @pl.when(temporal == most)
    def _():
        own(range(least, least + handed))

    @pl.when(temporal != most)
    def _():
        for slot in range(handed):
            put(least + slot, [given_ref.at[slot, part] for part in range(3)])


def frames_held(ranks):
    me = lax.axis_index("tm")
    return [me ^ step for step in distances(ranks)]


def fill_bias(bias_ref, mask_ref, frames, blocks):
    row = lax.broadcasted_iota(jnp.int32, (ROWS, bias_ref.shape[1]), 0)
    column = lax.broadcasted_iota(jnp.int32, (ROWS, bias_ref.shape[1]), 1)
    span = len(frames) // blocks
    for step, own in enumerate(frames):
        strip = jnp.zeros(row.shape, jnp.int32)
        for column_step, other in enumerate(frames):
            strip = jnp.where(column // ROWS == column_step, mask_ref[own // span, other // span], strip)
        kept = jnp.logical_and(column % ROWS == row, strip == 1)
        bias_ref[step * ROWS : (step + 1) * ROWS, :] = jnp.where(kept, jnp.float32(0.0), jnp.float32(NEGATIVE))


def temporal_kernel(sizes, bias_ref, *rest):
    slots, ranks, share = sizes
    in_refs, out_ref = rest[:ranks], rest[ranks]
    frames = frames_held(ranks)
    for slot in range(slots):
        groups = [pl.ds(start, ROWS) for start in range(0, share, ROWS)]
        triples = [
            [jnp.concatenate([ref[slot, part, rows, :] for ref in in_refs], axis=0) for part in range(3)]
            for rows in groups
        ]
        for rows, blended in zip(groups, attend(triples, bias_ref[...])):
            for step, frame in enumerate(frames):
                out_ref[frame, slot, rows, :] = blended[step * ROWS : (step + 1) * ROWS]


def head_copies(ref, out_ref, order_ref, slots, ref_slot):
    return [(ref.at[:, ref_slot(slot)], out_ref.at[order_ref[slot]]) for slot in slots]


def own_kernel(sizes, class_ref, spatial_ref, back_ref, out_ref, order_ref, sems):
    group_heads, most, least = sizes
    temporal = rank_heads(class_ref, order_ref, group_heads)

    def run(count, slots):
        copies = head_copies(back_ref, out_ref, order_ref, slots, lambda slot: slot)
        for slot in range(group_heads - count):
            head = order_ref[group_heads + slot]
            copies.append((spatial_ref.at[head], out_ref.at[head]))
        copy_all(copies, sems)()

    @pl.when(temporal == most)
    def _():
        run(most, range(least + (most - least) // 2))

    @pl.when(temporal != most)
    def _():
        run(least, range(least))


def merge_kernel(sizes, class_ref, back_ref, whole_ref, out_ref, order_ref, sems):
    group_heads, most, least = sizes
    handed = (most - least) // 2
    temporal = rank_heads(class_ref, order_ref, group_heads)

    @pl.when(temporal == most)
    def _():
        slots = range(least + handed, most)
        copy_all(head_copies(back_ref, out_ref, order_ref, slots, lambda slot: slot - handed), sems)()


def per_device(head_total, queries, key_vectors, value_vectors, head_class, frame_mask):
    ranks = lax.axis_size("tm")
    group_heads = queries.shape[2]
    patches, width = queries.shape[1], queries.shape[3]
    share = patches // ranks
    least = group_heads // 2 - group_heads // 3
    most = group_heads // 2 + group_heads // 3
    handed = (most - least) // 2
    slots = least + handed
    blocks = frame_mask.shape[0]
    smem = pl.BlockSpec(memory_space=pltpu.SMEM)
    vmem = pl.BlockSpec(memory_space=pltpu.VMEM)
    hbm = pl.BlockSpec(memory_space=pltpu.HBM)
    params = pltpu.CompilerParams(vmem_limit_bytes=16 * 2**20)

    order = pltpu.SMEM((2 * group_heads,), jnp.int32)
    q, k, v = (jnp.moveaxis(a[0], 1, 0) for a in (queries, key_vectors, value_vectors))
    pairs = [(h, h ^ 1) for h in range(head_total)]
    whole = jax.ShapeDtypeStruct(q.shape, q.dtype)
    steps = distances(ranks)
    by_rank = jax.ShapeDtypeStruct((group_heads, ranks, share, width), q.dtype)
    packed_shape = [jax.ShapeDtypeStruct((slots, 3, share, width), q.dtype)] * ranks
    cost = pl.CostEstimate(
        flops=4 * most * patches * patches * width,
        bytes_accessed=4 * q.size * 2,
        transcendentals=most * patches * patches,
    )

    def swap(array):
        return lax.ppermute(array, "head", pairs)

    def exchange(array):
        return lax.all_to_all(array, "tm", split_axis=0, concat_axis=0, tiled=True)

    def send(array, step):
        return lax.ppermute(array, "tm", [(rank, rank ^ step) for rank in range(ranks)])

    handed_heads, token = pl.pallas_call(
        functools.partial(hand_kernel, (group_heads, most, least)),
        out_shape=[
            jax.ShapeDtypeStruct((handed, 3, patches, width), q.dtype),
            jax.ShapeDtypeStruct((8, width), jnp.float32),
        ],
        in_specs=[smem] + [hbm] * 3,
        out_specs=[vmem] * 2,
        scratch_shapes=[order, pltpu.SemaphoreType.DMA((handed * 3,))],
        compiler_params=pltpu.CompilerParams(vmem_limit_bytes=53 * 2**20),
        name="hand",
    )(head_class, q, k, v)
    given = swap(handed_heads)
    q, k, v = pl.pallas_call(
        load_kernel,
        out_shape=[whole] * 3,
        in_specs=[hbm] * 3 + [vmem],
        out_specs=[vmem] * 3,
        scratch_shapes=[pltpu.SemaphoreType.DMA((3 * group_heads,))],
        compiler_params=pltpu.CompilerParams(vmem_limit_bytes=52 * 2**20),
        name="load",
    )(q, k, v, token)
    packed = pl.pallas_call(
        functools.partial(pack_kernel, (group_heads, most, least, ranks, share)),
        out_shape=packed_shape,
        in_specs=[smem] + [vmem] * 4,
        out_specs=[vmem] * ranks,
        scratch_shapes=[order],
        compiler_params=params,
        name="pack",
    )(head_class, q, k, v, given)
    arrived = [packed[0]] + [send(packed[step], step) for step in steps[1:]]
    spatial, bias = pl.pallas_call(
        functools.partial(spatial_kernel, (group_heads, ranks, blocks)),
        out_shape=[whole, jax.ShapeDtypeStruct((ranks * ROWS, ranks * ROWS), jnp.float32)],
        in_specs=[smem] * 2 + [vmem] * 3,
        out_specs=[vmem] * 2,
        scratch_shapes=[order],
        compiler_params=params,
        cost_estimate=cost,
        name="spatial",
    )(head_class, frame_mask, q, k, v)
    back = exchange(
        pl.pallas_call(
            functools.partial(temporal_kernel, (slots, ranks, share)),
            out_shape=jax.ShapeDtypeStruct((ranks, slots, share, width), q.dtype),
            in_specs=[vmem] * (1 + ranks),
            out_specs=vmem,
            compiler_params=params,
            name="temporal",
        )(bias, *arrived)
    )
    returned = swap(back)
    mostly = pl.pallas_call(
        functools.partial(own_kernel, (group_heads, most, least)),
        out_shape=by_rank,
        in_specs=[smem] + [vmem] * 2,
        out_specs=hbm,
        scratch_shapes=[order, pltpu.SemaphoreType.DMA((slots + group_heads,))],
        compiler_params=params,
        name="own",
    )(head_class, spatial.reshape(by_rank.shape), back)
    merged = pl.pallas_call(
        functools.partial(merge_kernel, (group_heads, most, least)),
        out_shape=by_rank,
        in_specs=[smem, vmem, hbm],
        out_specs=hbm,
        scratch_shapes=[order, pltpu.SemaphoreType.DMA((handed,))],
        input_output_aliases={2: 0},
        compiler_params=params,
        name="merge",
    )(head_class, returned, mostly)
    return jnp.moveaxis(merged.reshape(q.shape), 0, 1)[None]


def frame_attend(triple):
    query_block, key_block, value_block = triple
    scores = lax.dot_general(
        query_block, key_block, (((1,), (1,)), ((), ())), preferred_element_type=jnp.float32
    ) * (query_block.shape[-1] ** -0.5)
    exponent, totals = softmax_rows(scores)
    blended = jnp.dot(
        exponent.astype(jnp.bfloat16), value_block, preferred_element_type=jnp.float32
    )
    return (blended / totals).astype(jnp.bfloat16)


def run_spatial(triple):
    moved = tuple((jnp.moveaxis(a[0], 1, 0) for a in triple))
    blended = lax.map(frame_attend, moved)
    return jnp.moveaxis(blended, 0, 1)[None]


def run_temporal(triple, frame_mask):
    query_block, key_block, value_block = (
        lax.all_to_all(a, "tm", split_axis=1, concat_axis=0, tiled=True) for a in triple
    )
    score_scale = query_block.shape[-1] ** (-0.5)
    frame_total = query_block.shape[0]
    block_total = frame_mask.shape[0]
    frame_block = jnp.arange(frame_total, dtype=jnp.int32) // (frame_total // block_total)
    onehot = (frame_block[:, None] == jnp.arange(block_total, dtype=jnp.int32)[None, :]).astype(
        jnp.float32
    )
    allowed = jnp.dot(jnp.dot(onehot, frame_mask.astype(jnp.float32)), onehot.T) > 0.5
    scores = (
        jnp.einsum("fpmd,gpmd->pmfg", query_block, key_block, preferred_element_type=jnp.float32)
        * score_scale
    )
    scores = jnp.where(allowed, scores, jnp.float32(NEGATIVE))
    peak = jnp.max(scores, axis=-1, keepdims=True)
    exponent = jnp.where(allowed, jnp.exp(scores - peak), jnp.float32(0.0))
    totals = jnp.sum(exponent, axis=-1)
    blended = jnp.einsum(
        "pmfg,gpmd->fpmd",
        exponent.astype(jnp.bfloat16),
        value_block,
        preferred_element_type=jnp.float32,
    )
    result = (blended / jnp.transpose(totals, (2, 0, 1))[..., None]).astype(jnp.bfloat16)
    return lax.all_to_all(result, "tm", split_axis=0, concat_axis=1, tiled=True)


def per_device_many(queries, key_vectors, value_vectors, head_class, frame_mask):
    group_heads = queries.shape[2]
    moved_heads = group_heads // 3
    half_heads = group_heads // 2
    least_count = half_heads - moved_heads
    most_count = half_heads + moved_heads
    head_group = lax.axis_index("head")
    local_class = lax.dynamic_slice_in_dim(head_class, head_group * group_heads, group_heads)
    sorted_heads = jnp.argsort(local_class, stable=True)
    head_rank = jnp.argsort(sorted_heads)
    temporal_count = jnp.sum(local_class)
    position = jnp.arange(group_heads, dtype=jnp.int32)
    triple = (queries, key_vectors, value_vectors)
    spatial_in = tuple((jnp.take(a, sorted_heads[:most_count], axis=2) for a in triple))
    temporal_in = tuple((jnp.take(a, sorted_heads[least_count:], axis=2) for a in triple))
    spatial_out = run_spatial(spatial_in)
    temporal_out = run_temporal(temporal_in, frame_mask)
    result_pool = jnp.concatenate([spatial_out, temporal_out], axis=2)
    slot_index = jnp.where(
        position < group_heads - temporal_count, position, most_count + position - least_count
    )
    return jnp.take(result_pool, jnp.take(slot_index, head_rank), axis=2)


def solution(mesh):
    ranks, head_total = mesh.shape["tm"], mesh.shape["head"]
    spec = P("tm", None, "head", None)

    def whole(queries, key_vectors, value_vectors, head_class, frame_mask):
        few = (
            ranks & (ranks - 1) == 0
            and 2 <= ranks <= 8
            and queries.shape[0] == ranks
            and queries.shape[1] % (ranks * ROWS) == 0
            and head_total % 2 == 0
            and ranks % frame_mask.shape[0] == 0
        )
        body = functools.partial(per_device, head_total) if few else per_device_many
        return jax.shard_map(
            body, mesh=mesh, in_specs=(spec, spec, spec, P(), P()), out_specs=spec, check_vma=False
        )(queries, key_vectors, value_vectors, head_class, frame_mask)

    return whole
```

```python
import functools
import math

import jax
import jax.numpy as jnp
from jax import lax
from jax.experimental import pallas as pl
from jax.experimental.pallas import tpu as pltpu
from jax.sharding import PartitionSpec as P

ROWS = 16
NEGATIVE = -1e30


def rank_heads(class_ref, order_ref, group_heads, group=None):
    base = (lax.axis_index("head") if group is None else group) * group_heads
    temporal = jnp.int32(0)
    for head in range(group_heads):
        is_temporal = class_ref[base + head]
        slot = jnp.where(is_temporal == 1, temporal, group_heads + head - temporal)
        order_ref[slot] = jnp.int32(head)
        temporal = temporal + is_temporal
    return temporal


def softmax_rows(scores):
    peak = jnp.max(scores, axis=-1, keepdims=True)
    exponent = jnp.exp(scores - peak)
    return exponent, jnp.sum(exponent, axis=-1, keepdims=True)


def attend(triples, bias=None):
    factor = triples[0][0].shape[-1] ** -0.5 * math.log2(math.e)
    scores = [
        lax.dot_general(query, key, (((1,), (1,)), ((), ())), preferred_element_type=jnp.float32)
        for query, key, _ in triples
    ]
    if bias is not None:
        scores = [score + bias for score in scores]
    peaks = [jnp.max(score, axis=-1, keepdims=True) for score in scores]
    exponents = [jnp.exp2((score - peak) * factor) for score, peak in zip(scores, peaks)]
    totals = [jnp.sum(exponent, axis=-1, keepdims=True) for exponent in exponents]
    blended = [
        jnp.dot(exponent.astype(jnp.bfloat16), value, preferred_element_type=jnp.float32)
        for exponent, (_, _, value) in zip(exponents, triples)
    ]
    return [(blend / total).astype(jnp.bfloat16) for blend, total in zip(blended, totals)]


def copy_all(copies, sems):
    started = [pltpu.make_async_copy(source, target, sems.at[i]) for i, (source, target) in enumerate(copies)]
    for copy in started:
        copy.start()

    def wait():
        for copy in started:
            copy.wait()

    return wait


def load_kernel(class_ref, q_ref, k_ref, v_ref, q_out, k_out, v_out, sems):
    copies = [
        (ref.at[head], out.at[head])
        for ref, out in ((q_ref, q_out), (k_ref, k_out), (v_ref, v_out))
        for head in range(ref.shape[0])
    ]
    copy_all(copies, sems)()


def spatial_kernel(sizes, class_ref, mask_ref, q_ref, k_ref, v_ref, out_ref, bias_ref, order_ref):
    group_heads, ranks, blocks = sizes
    temporal = rank_heads(class_ref, order_ref, group_heads)

    def body(slot, carry):
        head = order_ref[group_heads + slot]
        (out_ref[head],) = attend([(q_ref[head], k_ref[head], v_ref[head])])
        return carry

    lax.fori_loop(0, group_heads - temporal, body, 0)
    fill_bias(bias_ref, mask_ref, frames_held(ranks), blocks)


def distances(ranks):
    far, near = [*range(ranks // 2, ranks, 2), *range(ranks // 2 + 1, ranks, 2)], list(range(1, ranks // 2))[::-1]
    return [0, *far[:1], *near[-2:-1], *far[1:3], *near[:-2], *near[-1:], *far[3:]]


def pack_kernel(sizes, class_ref, *refs):
    group_heads, most, least, ranks, share = sizes
    handed = (most - least) // 2
    own_refs, other_refs, out_refs, order_ref = refs[:3], refs[3:6], refs[6:-1], refs[-1]
    temporal = rank_heads(class_ref, order_ref, group_heads)
    me = lax.axis_index("tm")
    rows = [pl.ds(pl.multiple_of((me ^ step) * share, ROWS), share) for step in range(ranks)]

    def put(slots, refs, ref_slot):
        for slot in slots:
            head = order_ref[ref_slot(slot)]
            for part, ref in enumerate(refs):
                for step in range(ranks):
                    out_refs[step][slot, part] = ref[head, rows[step], :]

    put(range(least), own_refs, lambda slot: slot)

    @pl.when(temporal == most)
    def _():
        put(range(least, least + handed), own_refs, lambda slot: slot)

    @pl.when(temporal != most)
    def _():
        rank_heads(class_ref, order_ref, group_heads, lax.axis_index("head") ^ 1)
        put(range(least, least + handed), other_refs, lambda slot: slot - least + most - handed)


def frames_held(ranks):
    me = lax.axis_index("tm")
    return [me ^ step for step in distances(ranks)]


def fill_bias(bias_ref, mask_ref, frames, blocks):
    row = lax.broadcasted_iota(jnp.int32, (ROWS, bias_ref.shape[1]), 0)
    column = lax.broadcasted_iota(jnp.int32, (ROWS, bias_ref.shape[1]), 1)
    span = len(frames) // blocks
    for step, own in enumerate(frames):
        strip = jnp.zeros(row.shape, jnp.int32)
        for column_step, other in enumerate(frames):
            strip = jnp.where(column // ROWS == column_step, mask_ref[own // span, other // span], strip)
        kept = jnp.logical_and(column % ROWS == row, strip == 1)
        bias_ref[step * ROWS : (step + 1) * ROWS, :] = jnp.where(kept, jnp.float32(0.0), jnp.float32(NEGATIVE))


def temporal_kernel(sizes, bias_ref, *rest):
    slots, ranks, share = sizes
    in_refs, out_ref = rest[:ranks], rest[ranks]
    frames = frames_held(ranks)
    for slot in range(slots):
        groups = [pl.ds(start, ROWS) for start in range(0, share, ROWS)]
        triples = [
            [jnp.concatenate([ref[slot, part, rows, :] for ref in in_refs], axis=0) for part in range(3)]
            for rows in groups
        ]
        for rows, blended in zip(groups, attend(triples, bias_ref[...])):
            for step, frame in enumerate(frames):
                out_ref[frame, slot, rows, :] = blended[step * ROWS : (step + 1) * ROWS]


def head_copies(ref, out_ref, order_ref, slots, ref_slot):
    return [(ref.at[:, ref_slot(slot)], out_ref.at[order_ref[slot]]) for slot in slots]


def own_kernel(sizes, class_ref, spatial_ref, back_ref, out_ref, order_ref, sems):
    group_heads, most, least = sizes
    temporal = rank_heads(class_ref, order_ref, group_heads)

    def run(count, slots):
        copies = head_copies(back_ref, out_ref, order_ref, slots, lambda slot: slot)
        for slot in range(group_heads - count):
            head = order_ref[group_heads + slot]
            copies.append((spatial_ref.at[head], out_ref.at[head]))
        copy_all(copies, sems)()

    @pl.when(temporal == most)
    def _():
        run(most, range(least + (most - least) // 2))

    @pl.when(temporal != most)
    def _():
        run(least, range(least))


def merge_kernel(sizes, class_ref, back_ref, whole_ref, out_ref, order_ref, sems):
    group_heads, most, least = sizes
    handed = (most - least) // 2
    temporal = rank_heads(class_ref, order_ref, group_heads)

    @pl.when(temporal == most)
    def _():
        slots = range(least + handed, most)
        copy_all(head_copies(back_ref, out_ref, order_ref, slots, lambda slot: slot - handed), sems)()


def per_device(head_total, queries, key_vectors, value_vectors, head_class, frame_mask):
    ranks = lax.axis_size("tm")
    group_heads = queries.shape[2]
    patches, width = queries.shape[1], queries.shape[3]
    share = patches // ranks
    least = group_heads // 2 - group_heads // 3
    most = group_heads // 2 + group_heads // 3
    handed = (most - least) // 2
    slots = least + handed
    blocks = frame_mask.shape[0]
    smem = pl.BlockSpec(memory_space=pltpu.SMEM)
    vmem = pl.BlockSpec(memory_space=pltpu.VMEM)
    hbm = pl.BlockSpec(memory_space=pltpu.HBM)
    params = pltpu.CompilerParams(vmem_limit_bytes=16 * 2**20)

    order = pltpu.SMEM((2 * group_heads,), jnp.int32)
    q, k, v = (jnp.moveaxis(a[0], 1, 0) for a in (queries, key_vectors, value_vectors))
    pairs = [(h, h ^ 1) for h in range(head_total)]
    whole = jax.ShapeDtypeStruct(q.shape, q.dtype)
    steps = distances(ranks)
    by_rank = jax.ShapeDtypeStruct((group_heads, ranks, share, width), q.dtype)
    packed_shape = [jax.ShapeDtypeStruct((slots, 3, share, width), q.dtype)] * ranks
    cost = pl.CostEstimate(
        flops=4 * most * patches * patches * width,
        bytes_accessed=4 * q.size * 2,
        transcendentals=most * patches * patches,
    )

    def swap(array):
        return lax.ppermute(array, "head", pairs)

    def exchange(array):
        return lax.all_to_all(array, "tm", split_axis=0, concat_axis=0, tiled=True)

    def send(array, step):
        return lax.ppermute(array, "tm", [(rank, rank ^ step) for rank in range(ranks)])

    others = [swap(array) for array in (q, k, v)]
    q, k, v = pl.pallas_call(
        load_kernel,
        out_shape=[whole] * 3,
        in_specs=[smem] + [hbm] * 3,
        out_specs=[vmem] * 3,
        scratch_shapes=[pltpu.SemaphoreType.DMA((3 * group_heads,))],
        compiler_params=pltpu.CompilerParams(vmem_limit_bytes=52 * 2**20),
        name="load",
    )(head_class, q, k, v)
    packed = pl.pallas_call(
        functools.partial(pack_kernel, (group_heads, most, least, ranks, share)),
        out_shape=packed_shape,
        in_specs=[smem] + [vmem] * 6,
        out_specs=[vmem] * ranks,
        scratch_shapes=[order],
        compiler_params=params,
        name="pack",
    )(head_class, q, k, v, *others)
    arrived = [packed[0]] + [send(packed[step], step) for step in steps[1:]]
    spatial, bias = pl.pallas_call(
        functools.partial(spatial_kernel, (group_heads, ranks, blocks)),
        out_shape=[whole, jax.ShapeDtypeStruct((ranks * ROWS, ranks * ROWS), jnp.float32)],
        in_specs=[smem] * 2 + [vmem] * 3,
        out_specs=[vmem] * 2,
        scratch_shapes=[order],
        compiler_params=params,
        cost_estimate=cost,
        name="spatial",
    )(head_class, frame_mask, q, k, v)
    back = exchange(
        pl.pallas_call(
            functools.partial(temporal_kernel, (slots, ranks, share)),
            out_shape=jax.ShapeDtypeStruct((ranks, slots, share, width), q.dtype),
            in_specs=[vmem] * (1 + ranks),
            out_specs=vmem,
            compiler_params=params,
            name="temporal",
        )(bias, *arrived)
    )
    returned = swap(back)
    mostly = pl.pallas_call(
        functools.partial(own_kernel, (group_heads, most, least)),
        out_shape=by_rank,
        in_specs=[smem] + [vmem] * 2,
        out_specs=hbm,
        scratch_shapes=[order, pltpu.SemaphoreType.DMA((slots + group_heads,))],
        compiler_params=params,
        name="own",
    )(head_class, spatial.reshape(by_rank.shape), back)
    merged = pl.pallas_call(
        functools.partial(merge_kernel, (group_heads, most, least)),
        out_shape=by_rank,
        in_specs=[smem, vmem, hbm],
        out_specs=hbm,
        scratch_shapes=[order, pltpu.SemaphoreType.DMA((handed,))],
        input_output_aliases={2: 0},
        compiler_params=params,
        name="merge",
    )(head_class, returned, mostly)
    return jnp.moveaxis(merged.reshape(q.shape), 0, 1)[None]


def frame_attend(triple):
    query_block, key_block, value_block = triple
    scores = lax.dot_general(
        query_block, key_block, (((1,), (1,)), ((), ())), preferred_element_type=jnp.float32
    ) * (query_block.shape[-1] ** -0.5)
    exponent, totals = softmax_rows(scores)
    blended = jnp.dot(
        exponent.astype(jnp.bfloat16), value_block, preferred_element_type=jnp.float32
    )
    return (blended / totals).astype(jnp.bfloat16)


def run_spatial(triple):
    moved = tuple((jnp.moveaxis(a[0], 1, 0) for a in triple))
    blended = lax.map(frame_attend, moved)
    return jnp.moveaxis(blended, 0, 1)[None]


def run_temporal(triple, frame_mask):
    query_block, key_block, value_block = (
        lax.all_to_all(a, "tm", split_axis=1, concat_axis=0, tiled=True) for a in triple
    )
    score_scale = query_block.shape[-1] ** (-0.5)
    frame_total = query_block.shape[0]
    block_total = frame_mask.shape[0]
    frame_block = jnp.arange(frame_total, dtype=jnp.int32) // (frame_total // block_total)
    onehot = (frame_block[:, None] == jnp.arange(block_total, dtype=jnp.int32)[None, :]).astype(
        jnp.float32
    )
    allowed = jnp.dot(jnp.dot(onehot, frame_mask.astype(jnp.float32)), onehot.T) > 0.5
    scores = (
        jnp.einsum("fpmd,gpmd->pmfg", query_block, key_block, preferred_element_type=jnp.float32)
        * score_scale
    )
    scores = jnp.where(allowed, scores, jnp.float32(NEGATIVE))
    peak = jnp.max(scores, axis=-1, keepdims=True)
    exponent = jnp.where(allowed, jnp.exp(scores - peak), jnp.float32(0.0))
    totals = jnp.sum(exponent, axis=-1)
    blended = jnp.einsum(
        "pmfg,gpmd->fpmd",
        exponent.astype(jnp.bfloat16),
        value_block,
        preferred_element_type=jnp.float32,
    )
    result = (blended / jnp.transpose(totals, (2, 0, 1))[..., None]).astype(jnp.bfloat16)
    return lax.all_to_all(result, "tm", split_axis=0, concat_axis=1, tiled=True)


def per_device_many(queries, key_vectors, value_vectors, head_class, frame_mask):
    group_heads = queries.shape[2]
    moved_heads = group_heads // 3
    half_heads = group_heads // 2
    least_count = half_heads - moved_heads
    most_count = half_heads + moved_heads
    head_group = lax.axis_index("head")
    local_class = lax.dynamic_slice_in_dim(head_class, head_group * group_heads, group_heads)
    sorted_heads = jnp.argsort(local_class, stable=True)
    head_rank = jnp.argsort(sorted_heads)
    temporal_count = jnp.sum(local_class)
    position = jnp.arange(group_heads, dtype=jnp.int32)
    triple = (queries, key_vectors, value_vectors)
    spatial_in = tuple((jnp.take(a, sorted_heads[:most_count], axis=2) for a in triple))
    temporal_in = tuple((jnp.take(a, sorted_heads[least_count:], axis=2) for a in triple))
    spatial_out = run_spatial(spatial_in)
    temporal_out = run_temporal(temporal_in, frame_mask)
    result_pool = jnp.concatenate([spatial_out, temporal_out], axis=2)
    slot_index = jnp.where(
        position < group_heads - temporal_count, position, most_count + position - least_count
    )
    return jnp.take(result_pool, jnp.take(slot_index, head_rank), axis=2)


def solution(mesh):
    ranks, head_total = mesh.shape["tm"], mesh.shape["head"]
    spec = P("tm", None, "head", None)

    def whole(queries, key_vectors, value_vectors, head_class, frame_mask):
        few = (
            ranks & (ranks - 1) == 0
            and 2 <= ranks <= 8
            and queries.shape[0] == ranks
            and queries.shape[1] % (ranks * ROWS) == 0
            and head_total % 2 == 0
            and ranks % frame_mask.shape[0] == 0
        )
        body = functools.partial(per_device, head_total) if few else per_device_many
        return jax.shard_map(
            body, mesh=mesh, in_specs=(spec, spec, spec, P(), P()), out_specs=spec, check_vma=False
        )(queries, key_vectors, value_vectors, head_class, frame_mask)

    return whole
```

```python
import functools
import math

import jax
import jax.numpy as jnp
from jax import lax
from jax.experimental import pallas as pl
from jax.experimental.pallas import tpu as pltpu
from jax.sharding import PartitionSpec as P

ROWS = 16
NEGATIVE = -1e30


def rank_heads(class_ref, order_ref, group_heads, group=None):
    base = (lax.axis_index("head") if group is None else group) * group_heads
    temporal = jnp.int32(0)
    for head in range(group_heads):
        is_temporal = class_ref[base + head]
        slot = jnp.where(is_temporal == 1, temporal, group_heads + head - temporal)
        order_ref[slot] = jnp.int32(head)
        temporal = temporal + is_temporal
    return temporal


def softmax_rows(scores):
    peak = jnp.max(scores, axis=-1, keepdims=True)
    exponent = jnp.exp(scores - peak)
    return exponent, jnp.sum(exponent, axis=-1, keepdims=True)


def attend(triples, bias=None):
    factor = triples[0][0].shape[-1] ** -0.5 * math.log2(math.e)
    scores = [
        lax.dot_general(query, key, (((1,), (1,)), ((), ())), preferred_element_type=jnp.float32)
        for query, key, _ in triples
    ]
    if bias is not None:
        scores = [score + bias for score in scores]
    peaks = [jnp.max(score, axis=-1, keepdims=True) for score in scores]
    exponents = [jnp.exp2((score - peak) * factor) for score, peak in zip(scores, peaks)]
    totals = [jnp.sum(exponent, axis=-1, keepdims=True) for exponent in exponents]
    blended = [
        jnp.dot(exponent.astype(jnp.bfloat16), value, preferred_element_type=jnp.float32)
        for exponent, (_, _, value) in zip(exponents, triples)
    ]
    return [(blend / total).astype(jnp.bfloat16) for blend, total in zip(blended, totals)]


def copy_all(copies, sems):
    started = [pltpu.make_async_copy(source, target, sems.at[i]) for i, (source, target) in enumerate(copies)]
    for copy in started:
        copy.start()

    def wait():
        for copy in started:
            copy.wait()

    return wait


def load_kernel(class_ref, q_ref, k_ref, v_ref, q_out, k_out, v_out, sems):
    copies = [
        (ref.at[head], out.at[head])
        for ref, out in ((q_ref, q_out), (k_ref, k_out), (v_ref, v_out))
        for head in range(ref.shape[0])
    ]
    copy_all(copies, sems)()


def spatial_kernel(sizes, class_ref, mask_ref, q_ref, k_ref, v_ref, out_ref, bias_ref, order_ref):
    group_heads, ranks, blocks = sizes
    temporal = rank_heads(class_ref, order_ref, group_heads)

    def body(slot, carry):
        head = order_ref[group_heads + slot]
        (out_ref[head],) = attend([(q_ref[head], k_ref[head], v_ref[head])])
        return carry

    lax.fori_loop(0, group_heads - temporal, body, 0)
    fill_bias(bias_ref, mask_ref, frames_held(distances(ranks)), blocks)


def distances(ranks):
    far, near = [*range(ranks // 2, ranks, 2), *range(ranks // 2 + 1, ranks, 2)], list(range(1, ranks // 2))[::-1]
    return [0, *far[:1], *near[-2:-1], *far[1:2], *near[:-2], *near[-1:], *far[2:]]


def back_distances(ranks):
    far, near = list(range(ranks // 2, ranks)), list(range(1, ranks // 2))
    cut = len(far) // 2
    return [0, *far[cut:], *far[:cut], *near[1:], *near[:1]]


def block_rows(rank, share):
    return pl.ds(pl.multiple_of(rank * share, ROWS), share)


def pack_kernel(sizes, class_ref, *refs):
    group_heads, most, least, ranks, share = sizes
    handed = (most - least) // 2
    own_refs, other_refs, out_refs, order_ref = refs[:3], refs[3:6], refs[6:-1], refs[-1]
    temporal = rank_heads(class_ref, order_ref, group_heads)
    me = lax.axis_index("tm")
    rows = [block_rows(me ^ step, share) for step in range(ranks)]

    def put(slots, refs, ref_slot):
        for slot in slots:
            head = order_ref[ref_slot(slot)]
            for part, ref in enumerate(refs):
                for step in range(ranks):
                    out_refs[step][slot, part] = ref[head, rows[step], :]

    put(range(least), own_refs, lambda slot: slot)

    @pl.when(temporal == most)
    def _():
        put(range(least, least + handed), own_refs, lambda slot: slot)

    @pl.when(temporal != most)
    def _():
        rank_heads(class_ref, order_ref, group_heads, lax.axis_index("head") ^ 1)
        put(range(least, least + handed), other_refs, lambda slot: slot - least + most - handed)


def frames_held(steps):
    me = lax.axis_index("tm")
    return [me ^ step for step in steps]


def fill_bias(bias_ref, mask_ref, frames, blocks):
    row = lax.broadcasted_iota(jnp.int32, (ROWS, bias_ref.shape[1]), 0)
    column = lax.broadcasted_iota(jnp.int32, (ROWS, bias_ref.shape[1]), 1)
    span = len(frames) // blocks
    for step, own in enumerate(frames):
        strip = jnp.zeros(row.shape, jnp.int32)
        for column_step, other in enumerate(frames):
            strip = jnp.where(column // ROWS == column_step, mask_ref[own // span, other // span], strip)
        kept = jnp.logical_and(column % ROWS == row, strip == 1)
        bias_ref[step * ROWS : (step + 1) * ROWS, :] = jnp.where(kept, jnp.float32(0.0), jnp.float32(NEGATIVE))


def temporal_kernel(sizes, bias_ref, *rest):
    slots, ranks, share = sizes
    in_refs, out_refs = rest[:ranks], rest[ranks:]
    for slot in range(slots):
        groups = [pl.ds(start, ROWS) for start in range(0, share, ROWS)]
        triples = [
            [jnp.concatenate([ref[slot, part, rows, :] for ref in in_refs], axis=0) for part in range(3)]
            for rows in groups
        ]
        for rows, blended in zip(groups, attend(triples, bias_ref[...])):
            for at, out_ref in enumerate(out_refs):
                out_ref[slot, rows, :] = blended[at * ROWS : (at + 1) * ROWS]


def gather_kernel(sizes, *refs):
    least, ranks, share = sizes
    *back_refs, out_ref = refs
    for frame, back_ref in zip(frames_held(back_distances(ranks)), back_refs):
        for slot in range(out_ref.shape[0]):
            out_ref[slot, block_rows(frame, share), :] = back_ref[least + slot]


def own_kernel(sizes, class_ref, spatial_ref, *rest):
    group_heads, most, least, ranks, share = sizes
    back_refs = rest[:ranks]
    out_ref, order_ref, sems = rest[ranks:]
    temporal = rank_heads(class_ref, order_ref, group_heads)
    rows = [block_rows(frame, share) for frame in frames_held(back_distances(ranks))]

    def run(count, slots):
        copies = [
            (back_ref.at[slot], out_ref.at[order_ref[slot], block, :])
            for slot in slots
            for block, back_ref in zip(rows, back_refs)
        ]
        for slot in range(group_heads - count):
            head = order_ref[group_heads + slot]
            copies.append((spatial_ref.at[head], out_ref.at[head]))
        copy_all(copies, sems)()

    @pl.when(temporal == most)
    def _():
        run(most, range(least + (most - least) // 2))

    @pl.when(temporal != most)
    def _():
        run(least, range(least))


def merge_kernel(sizes, class_ref, given_ref, whole_ref, out_ref, order_ref, sems):
    group_heads, most, least = sizes
    handed = (most - least) // 2
    temporal = rank_heads(class_ref, order_ref, group_heads)

    @pl.when(temporal == most)
    def _():
        slots = range(handed)
        copy_all([(given_ref.at[slot], out_ref.at[order_ref[most - handed + slot]]) for slot in slots], sems)()


def per_device(head_total, queries, key_vectors, value_vectors, head_class, frame_mask):
    ranks = lax.axis_size("tm")
    group_heads = queries.shape[2]
    patches, width = queries.shape[1], queries.shape[3]
    share = patches // ranks
    least = group_heads // 2 - group_heads // 3
    most = group_heads // 2 + group_heads // 3
    handed = (most - least) // 2
    slots = least + handed
    blocks = frame_mask.shape[0]
    smem = pl.BlockSpec(memory_space=pltpu.SMEM)
    vmem = pl.BlockSpec(memory_space=pltpu.VMEM)
    hbm = pl.BlockSpec(memory_space=pltpu.HBM)
    params = pltpu.CompilerParams(vmem_limit_bytes=16 * 2**20)

    order = pltpu.SMEM((2 * group_heads,), jnp.int32)
    q, k, v = (jnp.moveaxis(a[0], 1, 0) for a in (queries, key_vectors, value_vectors))
    pairs = [(h, h ^ 1) for h in range(head_total)]
    whole = jax.ShapeDtypeStruct(q.shape, q.dtype)
    steps = distances(ranks)
    packed_shape = [jax.ShapeDtypeStruct((slots, 3, share, width), q.dtype)] * ranks
    cost = pl.CostEstimate(
        flops=4 * most * patches * patches * width,
        bytes_accessed=4 * q.size * 2,
        transcendentals=most * patches * patches,
    )

    def swap(array):
        return lax.ppermute(array, "head", pairs)

    def send(array, step):
        return lax.ppermute(array, "tm", [(rank, rank ^ step) for rank in range(ranks)])

    others = [swap(array) for array in (q, k, v)]
    q, k, v = pl.pallas_call(
        load_kernel,
        out_shape=[whole] * 3,
        in_specs=[smem] + [hbm] * 3,
        out_specs=[vmem] * 3,
        scratch_shapes=[pltpu.SemaphoreType.DMA((3 * group_heads,))],
        compiler_params=pltpu.CompilerParams(vmem_limit_bytes=52 * 2**20),
        name="load",
    )(head_class, q, k, v)
    packed = pl.pallas_call(
        functools.partial(pack_kernel, (group_heads, most, least, ranks, share)),
        out_shape=packed_shape,
        in_specs=[smem] + [vmem] * 6,
        out_specs=[vmem] * ranks,
        scratch_shapes=[order],
        compiler_params=params,
        name="pack",
    )(head_class, q, k, v, *others)
    arrived = [packed[0]] + [send(packed[step], step) for step in steps[1:]]
    spatial, bias = pl.pallas_call(
        functools.partial(spatial_kernel, (group_heads, ranks, blocks)),
        out_shape=[whole, jax.ShapeDtypeStruct((ranks * ROWS, ranks * ROWS), jnp.float32)],
        in_specs=[smem] * 2 + [vmem] * 3,
        out_specs=[vmem] * 2,
        scratch_shapes=[order],
        compiler_params=params,
        cost_estimate=cost,
        name="spatial",
    )(head_class, frame_mask, q, k, v)
    blended = pl.pallas_call(
        functools.partial(temporal_kernel, (slots, ranks, share)),
        out_shape=[jax.ShapeDtypeStruct((slots, share, width), q.dtype)] * ranks,
        in_specs=[vmem] * (1 + ranks),
        out_specs=[vmem] * ranks,
        compiler_params=params,
        name="temporal",
    )(bias, *arrived)
    by_step = dict(zip(steps, blended))
    back = [by_step[0]] + [send(by_step[step], step) for step in back_distances(ranks)[1:]]
    returned = swap(
        pl.pallas_call(
            functools.partial(gather_kernel, (least, ranks, share)),
            out_shape=jax.ShapeDtypeStruct((handed, patches, width), q.dtype),
            in_specs=[vmem] * ranks,
            out_specs=vmem,
            compiler_params=params,
            name="gather",
        )(*back)
    )
    mostly = pl.pallas_call(
        functools.partial(own_kernel, (group_heads, most, least, ranks, share)),
        out_shape=whole,
        in_specs=[smem] + [vmem] * (1 + ranks),
        out_specs=hbm,
        scratch_shapes=[order, pltpu.SemaphoreType.DMA((slots * ranks + group_heads,))],
        compiler_params=params,
        name="own",
    )(head_class, spatial, *back)
    merged = pl.pallas_call(
        functools.partial(merge_kernel, (group_heads, most, least)),
        out_shape=whole,
        in_specs=[smem, vmem, hbm],
        out_specs=hbm,
        scratch_shapes=[order, pltpu.SemaphoreType.DMA((handed,))],
        input_output_aliases={2: 0},
        compiler_params=params,
        name="merge",
    )(head_class, returned, mostly)
    return jnp.moveaxis(merged, 0, 1)[None]


def frame_attend(triple):
    query_block, key_block, value_block = triple
    scores = lax.dot_general(
        query_block, key_block, (((1,), (1,)), ((), ())), preferred_element_type=jnp.float32
    ) * (query_block.shape[-1] ** -0.5)
    exponent, totals = softmax_rows(scores)
    blended = jnp.dot(
        exponent.astype(jnp.bfloat16), value_block, preferred_element_type=jnp.float32
    )
    return (blended / totals).astype(jnp.bfloat16)


def run_spatial(triple):
    moved = tuple((jnp.moveaxis(a[0], 1, 0) for a in triple))
    blended = lax.map(frame_attend, moved)
    return jnp.moveaxis(blended, 0, 1)[None]


def run_temporal(triple, frame_mask):
    query_block, key_block, value_block = (
        lax.all_to_all(a, "tm", split_axis=1, concat_axis=0, tiled=True) for a in triple
    )
    score_scale = query_block.shape[-1] ** (-0.5)
    frame_total = query_block.shape[0]
    block_total = frame_mask.shape[0]
    frame_block = jnp.arange(frame_total, dtype=jnp.int32) // (frame_total // block_total)
    onehot = (frame_block[:, None] == jnp.arange(block_total, dtype=jnp.int32)[None, :]).astype(
        jnp.float32
    )
    allowed = jnp.dot(jnp.dot(onehot, frame_mask.astype(jnp.float32)), onehot.T) > 0.5
    scores = (
        jnp.einsum("fpmd,gpmd->pmfg", query_block, key_block, preferred_element_type=jnp.float32)
        * score_scale
    )
    scores = jnp.where(allowed, scores, jnp.float32(NEGATIVE))
    peak = jnp.max(scores, axis=-1, keepdims=True)
    exponent = jnp.where(allowed, jnp.exp(scores - peak), jnp.float32(0.0))
    totals = jnp.sum(exponent, axis=-1)
    blended = jnp.einsum(
        "pmfg,gpmd->fpmd",
        exponent.astype(jnp.bfloat16),
        value_block,
        preferred_element_type=jnp.float32,
    )
    result = (blended / jnp.transpose(totals, (2, 0, 1))[..., None]).astype(jnp.bfloat16)
    return lax.all_to_all(result, "tm", split_axis=0, concat_axis=1, tiled=True)


def per_device_many(queries, key_vectors, value_vectors, head_class, frame_mask):
    group_heads = queries.shape[2]
    moved_heads = group_heads // 3
    half_heads = group_heads // 2
    least_count = half_heads - moved_heads
    most_count = half_heads + moved_heads
    head_group = lax.axis_index("head")
    local_class = lax.dynamic_slice_in_dim(head_class, head_group * group_heads, group_heads)
    sorted_heads = jnp.argsort(local_class, stable=True)
    head_rank = jnp.argsort(sorted_heads)
    temporal_count = jnp.sum(local_class)
    position = jnp.arange(group_heads, dtype=jnp.int32)
    triple = (queries, key_vectors, value_vectors)
    spatial_in = tuple((jnp.take(a, sorted_heads[:most_count], axis=2) for a in triple))
    temporal_in = tuple((jnp.take(a, sorted_heads[least_count:], axis=2) for a in triple))
    spatial_out = run_spatial(spatial_in)
    temporal_out = run_temporal(temporal_in, frame_mask)
    result_pool = jnp.concatenate([spatial_out, temporal_out], axis=2)
    slot_index = jnp.where(
        position < group_heads - temporal_count, position, most_count + position - least_count
    )
    return jnp.take(result_pool, jnp.take(slot_index, head_rank), axis=2)


def solution(mesh):
    ranks, head_total = mesh.shape["tm"], mesh.shape["head"]
    spec = P("tm", None, "head", None)

    def whole(queries, key_vectors, value_vectors, head_class, frame_mask):
        few = (
            ranks & (ranks - 1) == 0
            and 2 <= ranks <= 8
            and queries.shape[0] == ranks
            and queries.shape[1] % (ranks * ROWS) == 0
            and head_total % 2 == 0
            and ranks % frame_mask.shape[0] == 0
        )
        body = functools.partial(per_device, head_total) if few else per_device_many
        return jax.shard_map(
            body, mesh=mesh, in_specs=(spec, spec, spec, P(), P()), out_specs=spec, check_vma=False
        )(queries, key_vectors, value_vectors, head_class, frame_mask)

    return whole
```

```python
import functools
import math

import jax
import jax.numpy as jnp
from jax import lax
from jax.experimental import pallas as pl
from jax.experimental.pallas import tpu as pltpu
from jax.sharding import PartitionSpec as P

ROWS = 16
NEGATIVE = -1e30


def rank_heads(class_ref, order_ref, group_heads, group=None):
    base = (lax.axis_index("head") if group is None else group) * group_heads
    temporal = jnp.int32(0)
    for head in range(group_heads):
        is_temporal = class_ref[base + head]
        slot = jnp.where(is_temporal == 1, temporal, group_heads + head - temporal)
        order_ref[slot] = jnp.int32(head)
        temporal = temporal + is_temporal
    return temporal


def softmax_rows(scores):
    peak = jnp.max(scores, axis=-1, keepdims=True)
    exponent = jnp.exp(scores - peak)
    return exponent, jnp.sum(exponent, axis=-1, keepdims=True)


def attend(triples, bias=None):
    factor = triples[0][0].shape[-1] ** -0.5 * math.log2(math.e)
    scores = [
        lax.dot_general(query, key, (((1,), (1,)), ((), ())), preferred_element_type=jnp.float32)
        for query, key, _ in triples
    ]
    if bias is not None:
        scores = [score + bias for score in scores]
    peaks = [jnp.max(score, axis=-1, keepdims=True) for score in scores]
    exponents = [jnp.exp2((score - peak) * factor) for score, peak in zip(scores, peaks)]
    totals = [jnp.sum(exponent, axis=-1, keepdims=True) for exponent in exponents]
    blended = [
        jnp.dot(exponent.astype(jnp.bfloat16), value, preferred_element_type=jnp.float32)
        for exponent, (_, _, value) in zip(exponents, triples)
    ]
    return [(blend / total).astype(jnp.bfloat16) for blend, total in zip(blended, totals)]


def copy_all(copies, sems):
    started = [pltpu.make_async_copy(source, target, sems.at[i]) for i, (source, target) in enumerate(copies)]
    for copy in started:
        copy.start()

    def wait():
        for copy in started:
            copy.wait()

    return wait


def load_kernel(class_ref, q_ref, k_ref, v_ref, q_out, k_out, v_out, sems):
    copies = [
        (ref.at[head], out.at[head])
        for ref, out in ((q_ref, q_out), (k_ref, k_out), (v_ref, v_out))
        for head in range(ref.shape[0])
    ]
    copy_all(copies, sems)()


def spatial_kernel(sizes, class_ref, mask_ref, q_ref, k_ref, v_ref, out_ref, bias_ref, order_ref):
    group_heads, ranks, blocks = sizes
    temporal = rank_heads(class_ref, order_ref, group_heads)

    def body(slot, carry):
        head = order_ref[group_heads + slot]
        (out_ref[head],) = attend([(q_ref[head], k_ref[head], v_ref[head])])
        return carry

    lax.fori_loop(0, group_heads - temporal, body, 0)
    fill_bias(bias_ref, mask_ref, frames_held(distances(ranks)), blocks)


def distances(ranks):
    far, near = [*range(ranks // 2, ranks, 2), *range(ranks // 2 + 1, ranks, 2)], list(range(1, ranks // 2))[::-1]
    return [0, *far[:1], *near[-2:-1], *far[1:2], *near[:-2], *near[-1:], *far[2:]]


def back_distances(ranks):
    far, near = list(range(ranks // 2, ranks)), list(range(1, ranks // 2))
    cut = len(far) // 2
    return [0, *far[cut:], *far[:cut], *near[1:], *near[:1]]


def block_rows(rank, share):
    return pl.ds(pl.multiple_of(rank * share, ROWS), share)


def pack_kernel(sizes, class_ref, *refs):
    group_heads, most, least, ranks, share = sizes
    handed = (most - least) // 2
    own_refs, other_refs, out_refs, order_ref = refs[:3], refs[3:6], refs[6:-1], refs[-1]
    temporal = rank_heads(class_ref, order_ref, group_heads)
    me = lax.axis_index("tm")
    rows = [block_rows(me ^ step, share) for step in range(ranks)]

    def put(slots, refs, ref_slot):
        for slot in slots:
            head = order_ref[ref_slot(slot)]
            for part, ref in enumerate(refs):
                for step in range(ranks):
                    out_refs[step][slot, part] = ref[head, rows[step], :]

    put(range(least), own_refs, lambda slot: slot)

    @pl.when(temporal == most)
    def _():
        put(range(least, least + handed), own_refs, lambda slot: slot)

    @pl.when(temporal != most)
    def _():
        rank_heads(class_ref, order_ref, group_heads, lax.axis_index("head") ^ 1)
        put(range(least, least + handed), other_refs, lambda slot: slot - least + most - handed)


def frames_held(steps):
    me = lax.axis_index("tm")
    return [me ^ step for step in steps]


def fill_bias(bias_ref, mask_ref, frames, blocks):
    row = lax.broadcasted_iota(jnp.int32, (ROWS, bias_ref.shape[1]), 0)
    column = lax.broadcasted_iota(jnp.int32, (ROWS, bias_ref.shape[1]), 1)
    span = len(frames) // blocks
    for step, own in enumerate(frames):
        strip = jnp.zeros(row.shape, jnp.int32)
        for column_step, other in enumerate(frames):
            strip = jnp.where(column // ROWS == column_step, mask_ref[own // span, other // span], strip)
        kept = jnp.logical_and(column % ROWS == row, strip == 1)
        bias_ref[step * ROWS : (step + 1) * ROWS, :] = jnp.where(kept, jnp.float32(0.0), jnp.float32(NEGATIVE))


def temporal_kernel(sizes, wanted, bias_ref, *rest):
    slots, ranks, share = sizes
    in_refs, out_refs = rest[:ranks], rest[ranks:]
    bias = jnp.concatenate([bias_ref[at * ROWS : (at + 1) * ROWS, :] for at in wanted], axis=0)
    for slot in range(slots):
        groups = [pl.ds(start, ROWS) for start in range(0, share, ROWS)]
        triples = [
            [
                jnp.concatenate([ref[slot, part, rows, :] for ref in refs], axis=0)
                for part, refs in enumerate(([in_refs[at] for at in wanted], in_refs, in_refs))
            ]
            for rows in groups
        ]
        for rows, blended in zip(groups, attend(triples, bias)):
            for at, out_ref in enumerate(out_refs):
                out_ref[slot, rows, :] = blended[at * ROWS : (at + 1) * ROWS]


def gather_kernel(sizes, *refs):
    least, ranks, share = sizes
    *back_refs, out_ref = refs
    for frame, back_ref in zip(frames_held(back_distances(ranks)), back_refs):
        for slot in range(out_ref.shape[0]):
            out_ref[slot, block_rows(frame, share), :] = back_ref[least + slot]


def own_kernel(sizes, class_ref, spatial_ref, *rest):
    group_heads, most, least, ranks, share = sizes
    back_refs = rest[:ranks]
    out_ref, order_ref, sems = rest[ranks:]
    temporal = rank_heads(class_ref, order_ref, group_heads)
    rows = [block_rows(frame, share) for frame in frames_held(back_distances(ranks))]

    def run(count, slots):
        copies = [
            (back_ref.at[slot], out_ref.at[order_ref[slot], block, :])
            for slot in slots
            for block, back_ref in zip(rows, back_refs)
        ]
        for slot in range(group_heads - count):
            head = order_ref[group_heads + slot]
            copies.append((spatial_ref.at[head], out_ref.at[head]))
        copy_all(copies, sems)()

    @pl.when(temporal == most)
    def _():
        run(most, range(least + (most - least) // 2))

    @pl.when(temporal != most)
    def _():
        run(least, range(least))


def merge_kernel(sizes, class_ref, given_ref, whole_ref, out_ref, order_ref, sems):
    group_heads, most, least = sizes
    handed = (most - least) // 2
    temporal = rank_heads(class_ref, order_ref, group_heads)

    @pl.when(temporal == most)
    def _():
        slots = range(handed)
        copy_all([(given_ref.at[slot], out_ref.at[order_ref[most - handed + slot]]) for slot in slots], sems)()


def per_device(head_total, queries, key_vectors, value_vectors, head_class, frame_mask):
    ranks = lax.axis_size("tm")
    group_heads = queries.shape[2]
    patches, width = queries.shape[1], queries.shape[3]
    share = patches // ranks
    least = group_heads // 2 - group_heads // 3
    most = group_heads // 2 + group_heads // 3
    handed = (most - least) // 2
    slots = least + handed
    blocks = frame_mask.shape[0]
    smem = pl.BlockSpec(memory_space=pltpu.SMEM)
    vmem = pl.BlockSpec(memory_space=pltpu.VMEM)
    hbm = pl.BlockSpec(memory_space=pltpu.HBM)
    params = pltpu.CompilerParams(vmem_limit_bytes=16 * 2**20)

    order = pltpu.SMEM((2 * group_heads,), jnp.int32)
    q, k, v = (jnp.moveaxis(a[0], 1, 0) for a in (queries, key_vectors, value_vectors))
    pairs = [(h, h ^ 1) for h in range(head_total)]
    whole = jax.ShapeDtypeStruct(q.shape, q.dtype)
    steps = distances(ranks)
    packed_shape = [jax.ShapeDtypeStruct((slots, 3, share, width), q.dtype)] * ranks
    cost = pl.CostEstimate(
        flops=4 * most * patches * patches * width,
        bytes_accessed=4 * q.size * 2,
        transcendentals=most * patches * patches,
    )

    def swap(array):
        return lax.ppermute(array, "head", pairs)

    def send(array, step):
        return lax.ppermute(array, "tm", [(rank, rank ^ step) for rank in range(ranks)])

    others = [swap(array) for array in (q, k, v)]
    q, k, v = pl.pallas_call(
        load_kernel,
        out_shape=[whole] * 3,
        in_specs=[smem] + [hbm] * 3,
        out_specs=[vmem] * 3,
        scratch_shapes=[pltpu.SemaphoreType.DMA((3 * group_heads,))],
        compiler_params=pltpu.CompilerParams(vmem_limit_bytes=52 * 2**20),
        name="load",
    )(head_class, q, k, v)
    packed = pl.pallas_call(
        functools.partial(pack_kernel, (group_heads, most, least, ranks, share)),
        out_shape=packed_shape,
        in_specs=[smem] + [vmem] * 6,
        out_specs=[vmem] * ranks,
        scratch_shapes=[order],
        compiler_params=params,
        name="pack",
    )(head_class, q, k, v, *others)
    arrived = [packed[0]] + [send(packed[step], step) for step in steps[1:]]
    spatial, bias = pl.pallas_call(
        functools.partial(spatial_kernel, (group_heads, ranks, blocks)),
        out_shape=[whole, jax.ShapeDtypeStruct((ranks * ROWS, ranks * ROWS), jnp.float32)],
        in_specs=[smem] * 2 + [vmem] * 3,
        out_specs=[vmem] * 2,
        scratch_shapes=[order],
        compiler_params=params,
        cost_estimate=cost,
        name="spatial",
    )(head_class, frame_mask, q, k, v)
    by_step = {}
    for name, far in (("temporal_far", True), ("temporal_near", False)):
        wanted = [at for at, step in enumerate(steps) if (step >= ranks // 2) == far]
        blended = pl.pallas_call(
            functools.partial(temporal_kernel, (slots, ranks, share), wanted),
            out_shape=[jax.ShapeDtypeStruct((slots, share, width), q.dtype)] * len(wanted),
            in_specs=[vmem] * (1 + ranks),
            out_specs=[vmem] * len(wanted),
            compiler_params=params,
            name=name,
        )(bias, *arrived)
        by_step.update((steps[at], array) for at, array in zip(wanted, blended))
    back = [by_step[0]] + [send(by_step[step], step) for step in back_distances(ranks)[1:]]
    returned = swap(
        pl.pallas_call(
            functools.partial(gather_kernel, (least, ranks, share)),
            out_shape=jax.ShapeDtypeStruct((handed, patches, width), q.dtype),
            in_specs=[vmem] * ranks,
            out_specs=vmem,
            compiler_params=params,
            name="gather",
        )(*back)
    )
    mostly = pl.pallas_call(
        functools.partial(own_kernel, (group_heads, most, least, ranks, share)),
        out_shape=whole,
        in_specs=[smem] + [vmem] * (1 + ranks),
        out_specs=hbm,
        scratch_shapes=[order, pltpu.SemaphoreType.DMA((slots * ranks + group_heads,))],
        compiler_params=params,
        name="own",
    )(head_class, spatial, *back)
    merged = pl.pallas_call(
        functools.partial(merge_kernel, (group_heads, most, least)),
        out_shape=whole,
        in_specs=[smem, vmem, hbm],
        out_specs=hbm,
        scratch_shapes=[order, pltpu.SemaphoreType.DMA((handed,))],
        input_output_aliases={2: 0},
        compiler_params=params,
        name="merge",
    )(head_class, returned, mostly)
    return jnp.moveaxis(merged, 0, 1)[None]


def frame_attend(triple):
    query_block, key_block, value_block = triple
    scores = lax.dot_general(
        query_block, key_block, (((1,), (1,)), ((), ())), preferred_element_type=jnp.float32
    ) * (query_block.shape[-1] ** -0.5)
    exponent, totals = softmax_rows(scores)
    blended = jnp.dot(
        exponent.astype(jnp.bfloat16), value_block, preferred_element_type=jnp.float32
    )
    return (blended / totals).astype(jnp.bfloat16)


def run_spatial(triple):
    moved = tuple((jnp.moveaxis(a[0], 1, 0) for a in triple))
    blended = lax.map(frame_attend, moved)
    return jnp.moveaxis(blended, 0, 1)[None]


def run_temporal(triple, frame_mask):
    query_block, key_block, value_block = (
        lax.all_to_all(a, "tm", split_axis=1, concat_axis=0, tiled=True) for a in triple
    )
    score_scale = query_block.shape[-1] ** (-0.5)
    frame_total = query_block.shape[0]
    block_total = frame_mask.shape[0]
    frame_block = jnp.arange(frame_total, dtype=jnp.int32) // (frame_total // block_total)
    onehot = (frame_block[:, None] == jnp.arange(block_total, dtype=jnp.int32)[None, :]).astype(
        jnp.float32
    )
    allowed = jnp.dot(jnp.dot(onehot, frame_mask.astype(jnp.float32)), onehot.T) > 0.5
    scores = (
        jnp.einsum("fpmd,gpmd->pmfg", query_block, key_block, preferred_element_type=jnp.float32)
        * score_scale
    )
    scores = jnp.where(allowed, scores, jnp.float32(NEGATIVE))
    peak = jnp.max(scores, axis=-1, keepdims=True)
    exponent = jnp.where(allowed, jnp.exp(scores - peak), jnp.float32(0.0))
    totals = jnp.sum(exponent, axis=-1)
    blended = jnp.einsum(
        "pmfg,gpmd->fpmd",
        exponent.astype(jnp.bfloat16),
        value_block,
        preferred_element_type=jnp.float32,
    )
    result = (blended / jnp.transpose(totals, (2, 0, 1))[..., None]).astype(jnp.bfloat16)
    return lax.all_to_all(result, "tm", split_axis=0, concat_axis=1, tiled=True)


def per_device_many(queries, key_vectors, value_vectors, head_class, frame_mask):
    group_heads = queries.shape[2]
    moved_heads = group_heads // 3
    half_heads = group_heads // 2
    least_count = half_heads - moved_heads
    most_count = half_heads + moved_heads
    head_group = lax.axis_index("head")
    local_class = lax.dynamic_slice_in_dim(head_class, head_group * group_heads, group_heads)
    sorted_heads = jnp.argsort(local_class, stable=True)
    head_rank = jnp.argsort(sorted_heads)
    temporal_count = jnp.sum(local_class)
    position = jnp.arange(group_heads, dtype=jnp.int32)
    triple = (queries, key_vectors, value_vectors)
    spatial_in = tuple((jnp.take(a, sorted_heads[:most_count], axis=2) for a in triple))
    temporal_in = tuple((jnp.take(a, sorted_heads[least_count:], axis=2) for a in triple))
    spatial_out = run_spatial(spatial_in)
    temporal_out = run_temporal(temporal_in, frame_mask)
    result_pool = jnp.concatenate([spatial_out, temporal_out], axis=2)
    slot_index = jnp.where(
        position < group_heads - temporal_count, position, most_count + position - least_count
    )
    return jnp.take(result_pool, jnp.take(slot_index, head_rank), axis=2)


def solution(mesh):
    ranks, head_total = mesh.shape["tm"], mesh.shape["head"]
    spec = P("tm", None, "head", None)

    def whole(queries, key_vectors, value_vectors, head_class, frame_mask):
        few = (
            ranks & (ranks - 1) == 0
            and 2 <= ranks <= 8
            and queries.shape[0] == ranks
            and queries.shape[1] % (ranks * ROWS) == 0
            and head_total % 2 == 0
            and ranks % frame_mask.shape[0] == 0
        )
        body = functools.partial(per_device, head_total) if few else per_device_many
        return jax.shard_map(
            body, mesh=mesh, in_specs=(spec, spec, spec, P(), P()), out_specs=spec, check_vma=False
        )(queries, key_vectors, value_vectors, head_class, frame_mask)

    return whole
```

```python
import functools
import math

import jax
import jax.numpy as jnp
from jax import lax
from jax.experimental import pallas as pl
from jax.experimental.pallas import tpu as pltpu
from jax.sharding import PartitionSpec as P

ROWS = 16
NEGATIVE = -1e30


def rank_heads(class_ref, order_ref, group_heads, group=None):
    base = (lax.axis_index("head") if group is None else group) * group_heads
    temporal = jnp.int32(0)
    for head in range(group_heads):
        is_temporal = class_ref[base + head]
        slot = jnp.where(is_temporal == 1, temporal, group_heads + head - temporal)
        order_ref[slot] = jnp.int32(head)
        temporal = temporal + is_temporal
    return temporal


def softmax_rows(scores):
    peak = jnp.max(scores, axis=-1, keepdims=True)
    exponent = jnp.exp(scores - peak)
    return exponent, jnp.sum(exponent, axis=-1, keepdims=True)


def attend(triples, bias=None):
    factor = triples[0][0].shape[-1] ** -0.5 * math.log2(math.e)
    scores = [
        lax.dot_general(query, key, (((1,), (1,)), ((), ())), preferred_element_type=jnp.float32)
        for query, key, _ in triples
    ]
    if bias is not None:
        scores = [score + bias for score in scores]
    peaks = [jnp.max(score, axis=-1, keepdims=True) for score in scores]
    exponents = [jnp.exp2((score - peak) * factor) for score, peak in zip(scores, peaks)]
    totals = [jnp.sum(exponent, axis=-1, keepdims=True) for exponent in exponents]
    blended = [
        jnp.dot(exponent.astype(jnp.bfloat16), value, preferred_element_type=jnp.float32)
        for exponent, (_, _, value) in zip(exponents, triples)
    ]
    return [(blend / total).astype(jnp.bfloat16) for blend, total in zip(blended, totals)]


def copy_all(copies, sems):
    started = [pltpu.make_async_copy(source, target, sems.at[i]) for i, (source, target) in enumerate(copies)]
    for copy in started:
        copy.start()

    def wait():
        for copy in started:
            copy.wait()

    return wait


def load_kernel(class_ref, q_ref, k_ref, v_ref, q_out, k_out, v_out, sems):
    copies = [
        (ref.at[head], out.at[head])
        for ref, out in ((q_ref, q_out), (k_ref, k_out), (v_ref, v_out))
        for head in range(ref.shape[0])
    ]
    copy_all(copies, sems)()


def spatial_kernel(sizes, class_ref, mask_ref, q_ref, k_ref, v_ref, out_ref, bias_ref, order_ref):
    group_heads, ranks, blocks = sizes
    temporal = rank_heads(class_ref, order_ref, group_heads)

    def body(slot, carry):
        head = order_ref[group_heads + slot]
        (out_ref[head],) = attend([(q_ref[head], k_ref[head], v_ref[head])])
        return carry

    lax.fori_loop(0, group_heads - temporal, body, 0)
    fill_bias(bias_ref, mask_ref, frames_held(distances(ranks)), blocks)


def distances(ranks):
    far, near = [*range(ranks // 2, ranks, 2), *range(ranks // 2 + 1, ranks, 2)], list(range(1, ranks // 2))[::-1]
    return [0, *far[:1], *near[-2:-1], *far[1:2], *near[:-2], *near[-1:], *far[2:]]


def back_distances(ranks):
    far, near = list(range(ranks // 2, ranks)), list(range(1, ranks // 2))
    cut = len(far) // 2
    return [0, *far[cut:], *far[:cut], *near[::-1]]


def block_rows(rank, share):
    return pl.ds(pl.multiple_of(rank * share, ROWS), share)


def pack_kernel(sizes, class_ref, *refs):
    group_heads, most, least, ranks, share = sizes
    handed = (most - least) // 2
    own_refs, other_refs, out_refs, order_ref = refs[:3], refs[3:6], refs[6:-1], refs[-1]
    temporal = rank_heads(class_ref, order_ref, group_heads)
    me = lax.axis_index("tm")
    rows = [block_rows(me ^ step, share) for step in range(ranks)]

    def put(slots, refs, ref_slot):
        for slot in slots:
            head = order_ref[ref_slot(slot)]
            for part, ref in enumerate(refs):
                for step in range(ranks):
                    out_refs[step][slot, part] = ref[head, rows[step], :]

    put(range(least), own_refs, lambda slot: slot)

    @pl.when(temporal == most)
    def _():
        put(range(least, least + handed), own_refs, lambda slot: slot)

    @pl.when(temporal != most)
    def _():
        rank_heads(class_ref, order_ref, group_heads, lax.axis_index("head") ^ 1)
        put(range(least, least + handed), other_refs, lambda slot: slot - least + most - handed)


def frames_held(steps):
    me = lax.axis_index("tm")
    return [me ^ step for step in steps]


def fill_bias(bias_ref, mask_ref, frames, blocks):
    row = lax.broadcasted_iota(jnp.int32, (ROWS, bias_ref.shape[1]), 0)
    column = lax.broadcasted_iota(jnp.int32, (ROWS, bias_ref.shape[1]), 1)
    span = len(frames) // blocks
    for step, own in enumerate(frames):
        strip = jnp.zeros(row.shape, jnp.int32)
        for column_step, other in enumerate(frames):
            strip = jnp.where(column // ROWS == column_step, mask_ref[own // span, other // span], strip)
        kept = jnp.logical_and(column % ROWS == row, strip == 1)
        bias_ref[step * ROWS : (step + 1) * ROWS, :] = jnp.where(kept, jnp.float32(0.0), jnp.float32(NEGATIVE))


def temporal_kernel(sizes, bias_ref, *rest):
    slots, ranks, share = sizes
    in_refs, out_refs = rest[:ranks], rest[ranks:]
    for slot in range(slots):
        groups = [pl.ds(start, ROWS) for start in range(0, share, ROWS)]
        triples = [
            [jnp.concatenate([ref[slot, part, rows, :] for ref in in_refs], axis=0) for part in range(3)]
            for rows in groups
        ]
        for rows, blended in zip(groups, attend(triples, bias_ref[...])):
            for at, out_ref in enumerate(out_refs):
                out_ref[slot, rows, :] = blended[at * ROWS : (at + 1) * ROWS]


def gather_kernel(sizes, *refs):
    least, ranks, share = sizes
    *back_refs, out_ref = refs
    for frame, back_ref in zip(frames_held(back_distances(ranks)), back_refs):
        for slot in range(out_ref.shape[0]):
            out_ref[slot, block_rows(frame, share), :] = back_ref[least + slot]


def own_kernel(sizes, class_ref, spatial_ref, *rest):
    group_heads, most, least, ranks, share = sizes
    back_refs = rest[:ranks]
    out_ref, order_ref, sems = rest[ranks:]
    temporal = rank_heads(class_ref, order_ref, group_heads)
    rows = [block_rows(frame, share) for frame in frames_held(back_distances(ranks))]

    def run(count, slots):
        copies = [
            (back_ref.at[slot], out_ref.at[order_ref[slot], block, :])
            for slot in slots
            for block, back_ref in zip(rows, back_refs)
        ]
        for slot in range(group_heads - count):
            head = order_ref[group_heads + slot]
            copies.append((spatial_ref.at[head], out_ref.at[head]))
        copy_all(copies, sems)()

    @pl.when(temporal == most)
    def _():
        run(most, range(least + (most - least) // 2))

    @pl.when(temporal != most)
    def _():
        run(least, range(least))


def merge_kernel(sizes, class_ref, given_ref, whole_ref, out_ref, order_ref, sems):
    group_heads, most, least = sizes
    handed = (most - least) // 2
    temporal = rank_heads(class_ref, order_ref, group_heads)

    @pl.when(temporal == most)
    def _():
        slots = range(handed)
        copy_all([(given_ref.at[slot], out_ref.at[order_ref[most - handed + slot]]) for slot in slots], sems)()


def per_device(head_total, queries, key_vectors, value_vectors, head_class, frame_mask):
    ranks = lax.axis_size("tm")
    group_heads = queries.shape[2]
    patches, width = queries.shape[1], queries.shape[3]
    share = patches // ranks
    least = group_heads // 2 - group_heads // 3
    most = group_heads // 2 + group_heads // 3
    handed = (most - least) // 2
    slots = least + handed
    blocks = frame_mask.shape[0]
    smem = pl.BlockSpec(memory_space=pltpu.SMEM)
    vmem = pl.BlockSpec(memory_space=pltpu.VMEM)
    hbm = pl.BlockSpec(memory_space=pltpu.HBM)
    params = pltpu.CompilerParams(vmem_limit_bytes=16 * 2**20)

    order = pltpu.SMEM((2 * group_heads,), jnp.int32)
    q, k, v = (jnp.moveaxis(a[0], 1, 0) for a in (queries, key_vectors, value_vectors))
    pairs = [(h, h ^ 1) for h in range(head_total)]
    whole = jax.ShapeDtypeStruct(q.shape, q.dtype)
    steps = distances(ranks)
    packed_shape = [jax.ShapeDtypeStruct((slots, 3, share, width), q.dtype)] * ranks
    cost = pl.CostEstimate(
        flops=4 * most * patches * patches * width,
        bytes_accessed=4 * q.size * 2,
        transcendentals=most * patches * patches,
    )

    def swap(array):
        return lax.ppermute(array, "head", pairs)

    def send(array, step):
        return lax.ppermute(array, "tm", [(rank, rank ^ step) for rank in range(ranks)])

    others = [swap(array) for array in (q, k, v)]
    q, k, v = pl.pallas_call(
        load_kernel,
        out_shape=[whole] * 3,
        in_specs=[smem] + [hbm] * 3,
        out_specs=[vmem] * 3,
        scratch_shapes=[pltpu.SemaphoreType.DMA((3 * group_heads,))],
        compiler_params=pltpu.CompilerParams(vmem_limit_bytes=52 * 2**20),
        name="load",
    )(head_class, q, k, v)
    packed = pl.pallas_call(
        functools.partial(pack_kernel, (group_heads, most, least, ranks, share)),
        out_shape=packed_shape,
        in_specs=[smem] + [vmem] * 6,
        out_specs=[vmem] * ranks,
        scratch_shapes=[order],
        compiler_params=params,
        name="pack",
    )(head_class, q, k, v, *others)
    arrived = [packed[0]] + [send(packed[step], step) for step in steps[1:]]
    spatial, bias = pl.pallas_call(
        functools.partial(spatial_kernel, (group_heads, ranks, blocks)),
        out_shape=[whole, jax.ShapeDtypeStruct((ranks * ROWS, ranks * ROWS), jnp.float32)],
        in_specs=[smem] * 2 + [vmem] * 3,
        out_specs=[vmem] * 2,
        scratch_shapes=[order],
        compiler_params=params,
        cost_estimate=cost,
        name="spatial",
    )(head_class, frame_mask, q, k, v)
    blended = pl.pallas_call(
        functools.partial(temporal_kernel, (slots, ranks, share)),
        out_shape=[jax.ShapeDtypeStruct((slots, share, width), q.dtype)] * ranks,
        in_specs=[vmem] * (1 + ranks),
        out_specs=[vmem] * ranks,
        compiler_params=params,
        name="temporal",
    )(bias, *arrived)
    by_step = dict(zip(steps, blended))
    back = [by_step[0]] + [send(by_step[step], step) for step in back_distances(ranks)[1:]]
    returned = swap(
        pl.pallas_call(
            functools.partial(gather_kernel, (least, ranks, share)),
            out_shape=jax.ShapeDtypeStruct((handed, patches, width), q.dtype),
            in_specs=[vmem] * ranks,
            out_specs=vmem,
            compiler_params=params,
            name="gather",
        )(*back)
    )
    mostly = pl.pallas_call(
        functools.partial(own_kernel, (group_heads, most, least, ranks, share)),
        out_shape=whole,
        in_specs=[smem] + [vmem] * (1 + ranks),
        out_specs=hbm,
        scratch_shapes=[order, pltpu.SemaphoreType.DMA((slots * ranks + group_heads,))],
        compiler_params=params,
        name="own",
    )(head_class, spatial, *back)
    merged = pl.pallas_call(
        functools.partial(merge_kernel, (group_heads, most, least)),
        out_shape=whole,
        in_specs=[smem, vmem, hbm],
        out_specs=hbm,
        scratch_shapes=[order, pltpu.SemaphoreType.DMA((handed,))],
        input_output_aliases={2: 0},
        compiler_params=params,
        name="merge",
    )(head_class, returned, mostly)
    return jnp.moveaxis(merged, 0, 1)[None]


def frame_attend(triple):
    query_block, key_block, value_block = triple
    scores = lax.dot_general(
        query_block, key_block, (((1,), (1,)), ((), ())), preferred_element_type=jnp.float32
    ) * (query_block.shape[-1] ** -0.5)
    exponent, totals = softmax_rows(scores)
    blended = jnp.dot(
        exponent.astype(jnp.bfloat16), value_block, preferred_element_type=jnp.float32
    )
    return (blended / totals).astype(jnp.bfloat16)


def run_spatial(triple):
    moved = tuple((jnp.moveaxis(a[0], 1, 0) for a in triple))
    blended = lax.map(frame_attend, moved)
    return jnp.moveaxis(blended, 0, 1)[None]


def run_temporal(triple, frame_mask):
    query_block, key_block, value_block = (
        lax.all_to_all(a, "tm", split_axis=1, concat_axis=0, tiled=True) for a in triple
    )
    score_scale = query_block.shape[-1] ** (-0.5)
    frame_total = query_block.shape[0]
    block_total = frame_mask.shape[0]
    frame_block = jnp.arange(frame_total, dtype=jnp.int32) // (frame_total // block_total)
    onehot = (frame_block[:, None] == jnp.arange(block_total, dtype=jnp.int32)[None, :]).astype(
        jnp.float32
    )
    allowed = jnp.dot(jnp.dot(onehot, frame_mask.astype(jnp.float32)), onehot.T) > 0.5
    scores = (
        jnp.einsum("fpmd,gpmd->pmfg", query_block, key_block, preferred_element_type=jnp.float32)
        * score_scale
    )
    scores = jnp.where(allowed, scores, jnp.float32(NEGATIVE))
    peak = jnp.max(scores, axis=-1, keepdims=True)
    exponent = jnp.where(allowed, jnp.exp(scores - peak), jnp.float32(0.0))
    totals = jnp.sum(exponent, axis=-1)
    blended = jnp.einsum(
        "pmfg,gpmd->fpmd",
        exponent.astype(jnp.bfloat16),
        value_block,
        preferred_element_type=jnp.float32,
    )
    result = (blended / jnp.transpose(totals, (2, 0, 1))[..., None]).astype(jnp.bfloat16)
    return lax.all_to_all(result, "tm", split_axis=0, concat_axis=1, tiled=True)


def per_device_many(queries, key_vectors, value_vectors, head_class, frame_mask):
    group_heads = queries.shape[2]
    moved_heads = group_heads // 3
    half_heads = group_heads // 2
    least_count = half_heads - moved_heads
    most_count = half_heads + moved_heads
    head_group = lax.axis_index("head")
    local_class = lax.dynamic_slice_in_dim(head_class, head_group * group_heads, group_heads)
    sorted_heads = jnp.argsort(local_class, stable=True)
    head_rank = jnp.argsort(sorted_heads)
    temporal_count = jnp.sum(local_class)
    position = jnp.arange(group_heads, dtype=jnp.int32)
    triple = (queries, key_vectors, value_vectors)
    spatial_in = tuple((jnp.take(a, sorted_heads[:most_count], axis=2) for a in triple))
    temporal_in = tuple((jnp.take(a, sorted_heads[least_count:], axis=2) for a in triple))
    spatial_out = run_spatial(spatial_in)
    temporal_out = run_temporal(temporal_in, frame_mask)
    result_pool = jnp.concatenate([spatial_out, temporal_out], axis=2)
    slot_index = jnp.where(
        position < group_heads - temporal_count, position, most_count + position - least_count
    )
    return jnp.take(result_pool, jnp.take(slot_index, head_rank), axis=2)


def solution(mesh):
    ranks, head_total = mesh.shape["tm"], mesh.shape["head"]
    spec = P("tm", None, "head", None)

    def whole(queries, key_vectors, value_vectors, head_class, frame_mask):
        few = (
            ranks & (ranks - 1) == 0
            and 2 <= ranks <= 8
            and queries.shape[0] == ranks
            and queries.shape[1] % (ranks * ROWS) == 0
            and head_total % 2 == 0
            and ranks % frame_mask.shape[0] == 0
        )
        body = functools.partial(per_device, head_total) if few else per_device_many
        return jax.shard_map(
            body, mesh=mesh, in_specs=(spec, spec, spec, P(), P()), out_specs=spec, check_vma=False
        )(queries, key_vectors, value_vectors, head_class, frame_mask)

    return whole
```

```python
import functools
import math

import jax
import jax.numpy as jnp
from jax import lax
from jax.experimental import pallas as pl
from jax.experimental.pallas import tpu as pltpu
from jax.sharding import PartitionSpec as P

ROWS = 16
NEGATIVE = -1e30


def rank_heads(class_ref, order_ref, group_heads, group=None):
    base = (lax.axis_index("head") if group is None else group) * group_heads
    temporal = jnp.int32(0)
    for head in range(group_heads):
        is_temporal = class_ref[base + head]
        slot = jnp.where(is_temporal == 1, temporal, group_heads + head - temporal)
        order_ref[slot] = jnp.int32(head)
        temporal = temporal + is_temporal
    return temporal


def softmax_rows(scores):
    peak = jnp.max(scores, axis=-1, keepdims=True)
    exponent = jnp.exp(scores - peak)
    return exponent, jnp.sum(exponent, axis=-1, keepdims=True)


def attend(triples, bias=None):
    factor = triples[0][0].shape[-1] ** -0.5 * math.log2(math.e)
    scores = [
        lax.dot_general(query, key, (((1,), (1,)), ((), ())), preferred_element_type=jnp.float32)
        for query, key, _ in triples
    ]
    if bias is not None:
        scores = [score + bias for score in scores]
    peaks = [jnp.max(score, axis=-1, keepdims=True) for score in scores]
    exponents = [jnp.exp2((score - peak) * factor) for score, peak in zip(scores, peaks)]
    totals = [jnp.sum(exponent, axis=-1, keepdims=True) for exponent in exponents]
    blended = [
        jnp.dot(exponent.astype(jnp.bfloat16), value, preferred_element_type=jnp.float32)
        for exponent, (_, _, value) in zip(exponents, triples)
    ]
    return [(blend / total).astype(jnp.bfloat16) for blend, total in zip(blended, totals)]


def copy_all(copies, sems):
    started = [pltpu.make_async_copy(source, target, sems.at[i]) for i, (source, target) in enumerate(copies)]
    for copy in started:
        copy.start()

    def wait():
        for copy in started:
            copy.wait()

    return wait


def load_kernel(class_ref, q_ref, k_ref, v_ref, q_out, k_out, v_out, sems):
    copies = [
        (ref.at[head], out.at[head])
        for ref, out in ((q_ref, q_out), (k_ref, k_out), (v_ref, v_out))
        for head in range(ref.shape[0])
    ]
    copy_all(copies, sems)()


def spatial_kernel(sizes, class_ref, mask_ref, q_ref, k_ref, v_ref, out_ref, bias_ref, order_ref):
    group_heads, ranks, blocks = sizes
    temporal = rank_heads(class_ref, order_ref, group_heads)

    def body(slot, carry):
        head = order_ref[group_heads + slot]
        (out_ref[head],) = attend([(q_ref[head], k_ref[head], v_ref[head])])
        return carry

    lax.fori_loop(0, group_heads - temporal, body, 0)
    fill_bias(bias_ref, mask_ref, frames_held(distances(ranks)), blocks)


def distances(ranks):
    far, near = list(range(ranks // 2, ranks)), list(range(1, ranks // 2))[::-1]
    return [0, *far[:1], *near[-2:-1], *far[1:2], *near[:-2], *near[-1:], *far[2:]]


def back_distances(ranks):
    far, near = list(range(ranks // 2, ranks)), list(range(1, ranks // 2))
    cut = len(far) // 2
    return [0, *far[cut:], *far[:cut], *near[::-1]]


def block_rows(rank, share):
    return pl.ds(pl.multiple_of(rank * share, ROWS), share)


def pack_kernel(sizes, class_ref, *refs):
    group_heads, most, least, ranks, share = sizes
    handed = (most - least) // 2
    own_refs, other_refs, out_refs, order_ref = refs[:3], refs[3:6], refs[6:-1], refs[-1]
    temporal = rank_heads(class_ref, order_ref, group_heads)
    me = lax.axis_index("tm")
    rows = [block_rows(me ^ step, share) for step in range(ranks)]

    def put(slots, refs, ref_slot):
        for slot in slots:
            head = order_ref[ref_slot(slot)]
            for part, ref in enumerate(refs):
                for step in range(ranks):
                    out_refs[step][slot, part] = ref[head, rows[step], :]

    put(range(least), own_refs, lambda slot: slot)

    @pl.when(temporal == most)
    def _():
        put(range(least, least + handed), own_refs, lambda slot: slot)

    @pl.when(temporal != most)
    def _():
        rank_heads(class_ref, order_ref, group_heads, lax.axis_index("head") ^ 1)
        put(range(least, least + handed), other_refs, lambda slot: slot - least + most - handed)


def frames_held(steps):
    me = lax.axis_index("tm")
    return [me ^ step for step in steps]


def fill_bias(bias_ref, mask_ref, frames, blocks):
    row = lax.broadcasted_iota(jnp.int32, (ROWS, bias_ref.shape[1]), 0)
    column = lax.broadcasted_iota(jnp.int32, (ROWS, bias_ref.shape[1]), 1)
    span = len(frames) // blocks
    for step, own in enumerate(frames):
        strip = jnp.zeros(row.shape, jnp.int32)
        for column_step, other in enumerate(frames):
            strip = jnp.where(column // ROWS == column_step, mask_ref[own // span, other // span], strip)
        kept = jnp.logical_and(column % ROWS == row, strip == 1)
        bias_ref[step * ROWS : (step + 1) * ROWS, :] = jnp.where(kept, jnp.float32(0.0), jnp.float32(NEGATIVE))


def temporal_kernel(sizes, bias_ref, *rest):
    slots, ranks, share = sizes
    in_refs, out_refs = rest[:ranks], rest[ranks:]
    for slot in range(slots):
        groups = [pl.ds(start, ROWS) for start in range(0, share, ROWS)]
        triples = [
            [jnp.concatenate([ref[slot, part, rows, :] for ref in in_refs], axis=0) for part in range(3)]
            for rows in groups
        ]
        for rows, blended in zip(groups, attend(triples, bias_ref[...])):
            for at, out_ref in enumerate(out_refs):
                out_ref[slot, rows, :] = blended[at * ROWS : (at + 1) * ROWS]


def gather_kernel(sizes, *refs):
    least, ranks, share = sizes
    *back_refs, out_ref = refs
    for frame, back_ref in zip(frames_held(back_distances(ranks)), back_refs):
        for slot in range(out_ref.shape[0]):
            out_ref[slot, block_rows(frame, share), :] = back_ref[least + slot]


def own_kernel(sizes, class_ref, spatial_ref, *rest):
    group_heads, most, least, ranks, share = sizes
    back_refs = rest[:ranks]
    out_ref, order_ref, sems = rest[ranks:]
    temporal = rank_heads(class_ref, order_ref, group_heads)
    rows = [block_rows(frame, share) for frame in frames_held(back_distances(ranks))]

    def run(count, slots):
        copies = [
            (back_ref.at[slot], out_ref.at[order_ref[slot], block, :])
            for slot in slots
            for block, back_ref in zip(rows, back_refs)
        ]
        for slot in range(group_heads - count):
            head = order_ref[group_heads + slot]
            copies.append((spatial_ref.at[head], out_ref.at[head]))
        copy_all(copies, sems)()

    @pl.when(temporal == most)
    def _():
        run(most, range(least + (most - least) // 2))

    @pl.when(temporal != most)
    def _():
        run(least, range(least))


def merge_kernel(sizes, class_ref, given_ref, whole_ref, out_ref, order_ref, sems):
    group_heads, most, least = sizes
    handed = (most - least) // 2
    temporal = rank_heads(class_ref, order_ref, group_heads)

    @pl.when(temporal == most)
    def _():
        slots = range(handed)
        copy_all([(given_ref.at[slot], out_ref.at[order_ref[most - handed + slot]]) for slot in slots], sems)()


def per_device(head_total, queries, key_vectors, value_vectors, head_class, frame_mask):
    ranks = lax.axis_size("tm")
    group_heads = queries.shape[2]
    patches, width = queries.shape[1], queries.shape[3]
    share = patches // ranks
    least = group_heads // 2 - group_heads // 3
    most = group_heads // 2 + group_heads // 3
    handed = (most - least) // 2
    slots = least + handed
    blocks = frame_mask.shape[0]
    smem = pl.BlockSpec(memory_space=pltpu.SMEM)
    vmem = pl.BlockSpec(memory_space=pltpu.VMEM)
    hbm = pl.BlockSpec(memory_space=pltpu.HBM)
    params = pltpu.CompilerParams(vmem_limit_bytes=16 * 2**20)

    order = pltpu.SMEM((2 * group_heads,), jnp.int32)
    q, k, v = (jnp.moveaxis(a[0], 1, 0) for a in (queries, key_vectors, value_vectors))
    pairs = [(h, h ^ 1) for h in range(head_total)]
    whole = jax.ShapeDtypeStruct(q.shape, q.dtype)
    steps = distances(ranks)
    packed_shape = [jax.ShapeDtypeStruct((slots, 3, share, width), q.dtype)] * ranks
    cost = pl.CostEstimate(
        flops=4 * most * patches * patches * width,
        bytes_accessed=4 * q.size * 2,
        transcendentals=most * patches * patches,
    )

    def swap(array):
        return lax.ppermute(array, "head", pairs)

    def send(array, step):
        return lax.ppermute(array, "tm", [(rank, rank ^ step) for rank in range(ranks)])

    others = [swap(array) for array in (q, k, v)]
    q, k, v = pl.pallas_call(
        load_kernel,
        out_shape=[whole] * 3,
        in_specs=[smem] + [hbm] * 3,
        out_specs=[vmem] * 3,
        scratch_shapes=[pltpu.SemaphoreType.DMA((3 * group_heads,))],
        compiler_params=pltpu.CompilerParams(vmem_limit_bytes=52 * 2**20),
        name="load",
    )(head_class, q, k, v)
    packed = pl.pallas_call(
        functools.partial(pack_kernel, (group_heads, most, least, ranks, share)),
        out_shape=packed_shape,
        in_specs=[smem] + [vmem] * 6,
        out_specs=[vmem] * ranks,
        scratch_shapes=[order],
        compiler_params=params,
        name="pack",
    )(head_class, q, k, v, *others)
    arrived = [packed[0]] + [send(packed[step], step) for step in steps[1:]]
    spatial, bias = pl.pallas_call(
        functools.partial(spatial_kernel, (group_heads, ranks, blocks)),
        out_shape=[whole, jax.ShapeDtypeStruct((ranks * ROWS, ranks * ROWS), jnp.float32)],
        in_specs=[smem] * 2 + [vmem] * 3,
        out_specs=[vmem] * 2,
        scratch_shapes=[order],
        compiler_params=params,
        cost_estimate=cost,
        name="spatial",
    )(head_class, frame_mask, q, k, v)
    blended = pl.pallas_call(
        functools.partial(temporal_kernel, (slots, ranks, share)),
        out_shape=[jax.ShapeDtypeStruct((slots, share, width), q.dtype)] * ranks,
        in_specs=[vmem] * (1 + ranks),
        out_specs=[vmem] * ranks,
        compiler_params=params,
        name="temporal",
    )(bias, *arrived)
    by_step = dict(zip(steps, blended))
    back = [by_step[0]] + [send(by_step[step], step) for step in back_distances(ranks)[1:]]
    returned = swap(
        pl.pallas_call(
            functools.partial(gather_kernel, (least, ranks, share)),
            out_shape=jax.ShapeDtypeStruct((handed, patches, width), q.dtype),
            in_specs=[vmem] * ranks,
            out_specs=vmem,
            compiler_params=params,
            name="gather",
        )(*back)
    )
    mostly = pl.pallas_call(
        functools.partial(own_kernel, (group_heads, most, least, ranks, share)),
        out_shape=whole,
        in_specs=[smem] + [vmem] * (1 + ranks),
        out_specs=hbm,
        scratch_shapes=[order, pltpu.SemaphoreType.DMA((slots * ranks + group_heads,))],
        compiler_params=params,
        name="own",
    )(head_class, spatial, *back)
    merged = pl.pallas_call(
        functools.partial(merge_kernel, (group_heads, most, least)),
        out_shape=whole,
        in_specs=[smem, vmem, hbm],
        out_specs=hbm,
        scratch_shapes=[order, pltpu.SemaphoreType.DMA((handed,))],
        input_output_aliases={2: 0},
        compiler_params=params,
        name="merge",
    )(head_class, returned, mostly)
    return jnp.moveaxis(merged, 0, 1)[None]


def frame_attend(triple):
    query_block, key_block, value_block = triple
    scores = lax.dot_general(
        query_block, key_block, (((1,), (1,)), ((), ())), preferred_element_type=jnp.float32
    ) * (query_block.shape[-1] ** -0.5)
    exponent, totals = softmax_rows(scores)
    blended = jnp.dot(
        exponent.astype(jnp.bfloat16), value_block, preferred_element_type=jnp.float32
    )
    return (blended / totals).astype(jnp.bfloat16)


def run_spatial(triple):
    moved = tuple((jnp.moveaxis(a[0], 1, 0) for a in triple))
    blended = lax.map(frame_attend, moved)
    return jnp.moveaxis(blended, 0, 1)[None]


def run_temporal(triple, frame_mask):
    query_block, key_block, value_block = (
        lax.all_to_all(a, "tm", split_axis=1, concat_axis=0, tiled=True) for a in triple
    )
    score_scale = query_block.shape[-1] ** (-0.5)
    frame_total = query_block.shape[0]
    block_total = frame_mask.shape[0]
    frame_block = jnp.arange(frame_total, dtype=jnp.int32) // (frame_total // block_total)
    onehot = (frame_block[:, None] == jnp.arange(block_total, dtype=jnp.int32)[None, :]).astype(
        jnp.float32
    )
    allowed = jnp.dot(jnp.dot(onehot, frame_mask.astype(jnp.float32)), onehot.T) > 0.5
    scores = (
        jnp.einsum("fpmd,gpmd->pmfg", query_block, key_block, preferred_element_type=jnp.float32)
        * score_scale
    )
    scores = jnp.where(allowed, scores, jnp.float32(NEGATIVE))
    peak = jnp.max(scores, axis=-1, keepdims=True)
    exponent = jnp.where(allowed, jnp.exp(scores - peak), jnp.float32(0.0))
    totals = jnp.sum(exponent, axis=-1)
    blended = jnp.einsum(
        "pmfg,gpmd->fpmd",
        exponent.astype(jnp.bfloat16),
        value_block,
        preferred_element_type=jnp.float32,
    )
    result = (blended / jnp.transpose(totals, (2, 0, 1))[..., None]).astype(jnp.bfloat16)
    return lax.all_to_all(result, "tm", split_axis=0, concat_axis=1, tiled=True)


def per_device_many(queries, key_vectors, value_vectors, head_class, frame_mask):
    group_heads = queries.shape[2]
    moved_heads = group_heads // 3
    half_heads = group_heads // 2
    least_count = half_heads - moved_heads
    most_count = half_heads + moved_heads
    head_group = lax.axis_index("head")
    local_class = lax.dynamic_slice_in_dim(head_class, head_group * group_heads, group_heads)
    sorted_heads = jnp.argsort(local_class, stable=True)
    head_rank = jnp.argsort(sorted_heads)
    temporal_count = jnp.sum(local_class)
    position = jnp.arange(group_heads, dtype=jnp.int32)
    triple = (queries, key_vectors, value_vectors)
    spatial_in = tuple((jnp.take(a, sorted_heads[:most_count], axis=2) for a in triple))
    temporal_in = tuple((jnp.take(a, sorted_heads[least_count:], axis=2) for a in triple))
    spatial_out = run_spatial(spatial_in)
    temporal_out = run_temporal(temporal_in, frame_mask)
    result_pool = jnp.concatenate([spatial_out, temporal_out], axis=2)
    slot_index = jnp.where(
        position < group_heads - temporal_count, position, most_count + position - least_count
    )
    return jnp.take(result_pool, jnp.take(slot_index, head_rank), axis=2)


def solution(mesh):
    ranks, head_total = mesh.shape["tm"], mesh.shape["head"]
    spec = P("tm", None, "head", None)

    def whole(queries, key_vectors, value_vectors, head_class, frame_mask):
        few = (
            ranks & (ranks - 1) == 0
            and 2 <= ranks <= 8
            and queries.shape[0] == ranks
            and queries.shape[1] % (ranks * ROWS) == 0
            and head_total % 2 == 0
            and ranks % frame_mask.shape[0] == 0
        )
        body = functools.partial(per_device, head_total) if few else per_device_many
        return jax.shard_map(
            body, mesh=mesh, in_specs=(spec, spec, spec, P(), P()), out_specs=spec, check_vma=False
        )(queries, key_vectors, value_vectors, head_class, frame_mask)

    return whole
```

```python
import functools
import math

import jax
import jax.numpy as jnp
from jax import lax
from jax.experimental import pallas as pl
from jax.experimental.pallas import tpu as pltpu
from jax.sharding import PartitionSpec as P

ROWS = 16
NEGATIVE = -1e30


def rank_heads(class_ref, order_ref, group_heads, group=None):
    base = (lax.axis_index("head") if group is None else group) * group_heads
    temporal = jnp.int32(0)
    for head in range(group_heads):
        is_temporal = class_ref[base + head]
        slot = jnp.where(is_temporal == 1, temporal, group_heads + head - temporal)
        order_ref[slot] = jnp.int32(head)
        temporal = temporal + is_temporal
    return temporal


def softmax_rows(scores):
    peak = jnp.max(scores, axis=-1, keepdims=True)
    exponent = jnp.exp(scores - peak)
    return exponent, jnp.sum(exponent, axis=-1, keepdims=True)


def attend(triples, bias=None):
    factor = triples[0][0].shape[-1] ** -0.5 * math.log2(math.e)
    scores = [
        lax.dot_general(query, key, (((1,), (1,)), ((), ())), preferred_element_type=jnp.float32)
        for query, key, _ in triples
    ]
    if bias is not None:
        scores = [score + bias for score in scores]
    peaks = [jnp.max(score, axis=-1, keepdims=True) for score in scores]
    exponents = [jnp.exp2((score - peak) * factor) for score, peak in zip(scores, peaks)]
    totals = [jnp.sum(exponent, axis=-1, keepdims=True) for exponent in exponents]
    blended = [
        jnp.dot(exponent.astype(jnp.bfloat16), value, preferred_element_type=jnp.float32)
        for exponent, (_, _, value) in zip(exponents, triples)
    ]
    return [(blend / total).astype(jnp.bfloat16) for blend, total in zip(blended, totals)]


def copy_all(copies, sems):
    started = [pltpu.make_async_copy(source, target, sems.at[i]) for i, (source, target) in enumerate(copies)]
    for copy in started:
        copy.start()

    def wait():
        for copy in started:
            copy.wait()

    return wait


def load_kernel(class_ref, q_ref, k_ref, v_ref, q_out, k_out, v_out, sems):
    copies = [
        (ref.at[head], out.at[head])
        for ref, out in ((q_ref, q_out), (k_ref, k_out), (v_ref, v_out))
        for head in range(ref.shape[0])
    ]
    copy_all(copies, sems)()


def spatial_kernel(sizes, class_ref, mask_ref, q_ref, k_ref, v_ref, out_ref, bias_ref, order_ref):
    group_heads, ranks, blocks = sizes
    temporal = rank_heads(class_ref, order_ref, group_heads)

    def body(slot, carry):
        head = order_ref[group_heads + slot]
        (out_ref[head],) = attend([(q_ref[head], k_ref[head], v_ref[head])])
        return carry

    lax.fori_loop(0, group_heads - temporal, body, 0)
    fill_bias(bias_ref, mask_ref, frames_held(distances(ranks)), blocks)


def distances(ranks):
    far, near = list(range(ranks // 2, ranks)), list(range(1, ranks // 2))[::-1]
    return [0, *far[:1], *near[-2:-1], *far[1:3], *near[:-2], *near[-1:], *far[3:]]


def back_distances(ranks):
    far, near = list(range(ranks // 2, ranks)), list(range(1, ranks // 2))
    cut = len(far) // 2
    return [0, *far[cut:], *far[:cut], *near[::-1]]


def block_rows(rank, share):
    return pl.ds(pl.multiple_of(rank * share, ROWS), share)


def pack_kernel(sizes, class_ref, *refs):
    group_heads, most, least, ranks, share = sizes
    handed = (most - least) // 2
    own_refs, other_refs, out_refs, order_ref = refs[:3], refs[3:6], refs[6:-1], refs[-1]
    temporal = rank_heads(class_ref, order_ref, group_heads)
    me = lax.axis_index("tm")
    rows = [block_rows(me ^ step, share) for step in range(ranks)]

    def put(slots, refs, ref_slot):
        for slot in slots:
            head = order_ref[ref_slot(slot)]
            for part, ref in enumerate(refs):
                for step in range(ranks):
                    out_refs[step][slot, part] = ref[head, rows[step], :]

    put(range(least), own_refs, lambda slot: slot)

    @pl.when(temporal == most)
    def _():
        put(range(least, least + handed), own_refs, lambda slot: slot)

    @pl.when(temporal != most)
    def _():
        rank_heads(class_ref, order_ref, group_heads, lax.axis_index("head") ^ 1)
        put(range(least, least + handed), other_refs, lambda slot: slot - least + most - handed)


def frames_held(steps):
    me = lax.axis_index("tm")
    return [me ^ step for step in steps]


def fill_bias(bias_ref, mask_ref, frames, blocks):
    row = lax.broadcasted_iota(jnp.int32, (ROWS, bias_ref.shape[1]), 0)
    column = lax.broadcasted_iota(jnp.int32, (ROWS, bias_ref.shape[1]), 1)
    span = len(frames) // blocks
    for step, own in enumerate(frames):
        strip = jnp.zeros(row.shape, jnp.int32)
        for column_step, other in enumerate(frames):
            strip = jnp.where(column // ROWS == column_step, mask_ref[own // span, other // span], strip)
        kept = jnp.logical_and(column % ROWS == row, strip == 1)
        bias_ref[step * ROWS : (step + 1) * ROWS, :] = jnp.where(kept, jnp.float32(0.0), jnp.float32(NEGATIVE))


def temporal_kernel(sizes, bias_ref, *rest):
    slots, ranks, share = sizes
    in_refs, out_refs = rest[:ranks], rest[ranks:]
    for slot in range(slots):
        groups = [pl.ds(start, ROWS) for start in range(0, share, ROWS)]
        triples = [
            [jnp.concatenate([ref[slot, part, rows, :] for ref in in_refs], axis=0) for part in range(3)]
            for rows in groups
        ]
        for rows, blended in zip(groups, attend(triples, bias_ref[...])):
            for at, out_ref in enumerate(out_refs):
                out_ref[slot, rows, :] = blended[at * ROWS : (at + 1) * ROWS]


def gather_kernel(sizes, *refs):
    least, ranks, share = sizes
    *back_refs, out_ref = refs
    for frame, back_ref in zip(frames_held(back_distances(ranks)), back_refs):
        for slot in range(out_ref.shape[0]):
            out_ref[slot, block_rows(frame, share), :] = back_ref[least + slot]


def own_kernel(sizes, class_ref, spatial_ref, *rest):
    group_heads, most, least, ranks, share = sizes
    back_refs = rest[:ranks]
    out_ref, order_ref, sems = rest[ranks:]
    temporal = rank_heads(class_ref, order_ref, group_heads)
    rows = [block_rows(frame, share) for frame in frames_held(back_distances(ranks))]

    def run(count, slots):
        copies = [
            (back_ref.at[slot], out_ref.at[order_ref[slot], block, :])
            for slot in slots
            for block, back_ref in zip(rows, back_refs)
        ]
        for slot in range(group_heads - count):
            head = order_ref[group_heads + slot]
            copies.append((spatial_ref.at[head], out_ref.at[head]))
        copy_all(copies, sems)()

    @pl.when(temporal == most)
    def _():
        run(most, range(least + (most - least) // 2))

    @pl.when(temporal != most)
    def _():
        run(least, range(least))


def merge_kernel(sizes, class_ref, given_ref, whole_ref, out_ref, order_ref, sems):
    group_heads, most, least = sizes
    handed = (most - least) // 2
    temporal = rank_heads(class_ref, order_ref, group_heads)

    @pl.when(temporal == most)
    def _():
        slots = range(handed)
        copy_all([(given_ref.at[slot], out_ref.at[order_ref[most - handed + slot]]) for slot in slots], sems)()


def per_device(head_total, queries, key_vectors, value_vectors, head_class, frame_mask):
    ranks = lax.axis_size("tm")
    group_heads = queries.shape[2]
    patches, width = queries.shape[1], queries.shape[3]
    share = patches // ranks
    least = group_heads // 2 - group_heads // 3
    most = group_heads // 2 + group_heads // 3
    handed = (most - least) // 2
    slots = least + handed
    blocks = frame_mask.shape[0]
    smem = pl.BlockSpec(memory_space=pltpu.SMEM)
    vmem = pl.BlockSpec(memory_space=pltpu.VMEM)
    hbm = pl.BlockSpec(memory_space=pltpu.HBM)
    params = pltpu.CompilerParams(vmem_limit_bytes=16 * 2**20)

    order = pltpu.SMEM((2 * group_heads,), jnp.int32)
    q, k, v = (jnp.moveaxis(a[0], 1, 0) for a in (queries, key_vectors, value_vectors))
    pairs = [(h, h ^ 1) for h in range(head_total)]
    whole = jax.ShapeDtypeStruct(q.shape, q.dtype)
    steps = distances(ranks)
    packed_shape = [jax.ShapeDtypeStruct((slots, 3, share, width), q.dtype)] * ranks
    cost = pl.CostEstimate(
        flops=4 * most * patches * patches * width,
        bytes_accessed=4 * q.size * 2,
        transcendentals=most * patches * patches,
    )

    def swap(array):
        return lax.ppermute(array, "head", pairs)

    def send(array, step):
        return lax.ppermute(array, "tm", [(rank, rank ^ step) for rank in range(ranks)])

    others = [swap(array) for array in (q, k, v)]
    q, k, v = pl.pallas_call(
        load_kernel,
        out_shape=[whole] * 3,
        in_specs=[smem] + [hbm] * 3,
        out_specs=[vmem] * 3,
        scratch_shapes=[pltpu.SemaphoreType.DMA((3 * group_heads,))],
        compiler_params=pltpu.CompilerParams(vmem_limit_bytes=52 * 2**20),
        name="load",
    )(head_class, q, k, v)
    packed = pl.pallas_call(
        functools.partial(pack_kernel, (group_heads, most, least, ranks, share)),
        out_shape=packed_shape,
        in_specs=[smem] + [vmem] * 6,
        out_specs=[vmem] * ranks,
        scratch_shapes=[order],
        compiler_params=params,
        name="pack",
    )(head_class, q, k, v, *others)
    arrived = [packed[0]] + [send(packed[step], step) for step in steps[1:]]
    spatial, bias = pl.pallas_call(
        functools.partial(spatial_kernel, (group_heads, ranks, blocks)),
        out_shape=[whole, jax.ShapeDtypeStruct((ranks * ROWS, ranks * ROWS), jnp.float32)],
        in_specs=[smem] * 2 + [vmem] * 3,
        out_specs=[vmem] * 2,
        scratch_shapes=[order],
        compiler_params=params,
        cost_estimate=cost,
        name="spatial",
    )(head_class, frame_mask, q, k, v)
    blended = pl.pallas_call(
        functools.partial(temporal_kernel, (slots, ranks, share)),
        out_shape=[jax.ShapeDtypeStruct((slots, share, width), q.dtype)] * ranks,
        in_specs=[vmem] * (1 + ranks),
        out_specs=[vmem] * ranks,
        compiler_params=params,
        name="temporal",
    )(bias, *arrived)
    by_step = dict(zip(steps, blended))
    back = [by_step[0]] + [send(by_step[step], step) for step in back_distances(ranks)[1:]]
    returned = swap(
        pl.pallas_call(
            functools.partial(gather_kernel, (least, ranks, share)),
            out_shape=jax.ShapeDtypeStruct((handed, patches, width), q.dtype),
            in_specs=[vmem] * ranks,
            out_specs=vmem,
            compiler_params=params,
            name="gather",
        )(*back)
    )
    mostly = pl.pallas_call(
        functools.partial(own_kernel, (group_heads, most, least, ranks, share)),
        out_shape=whole,
        in_specs=[smem] + [vmem] * (1 + ranks),
        out_specs=hbm,
        scratch_shapes=[order, pltpu.SemaphoreType.DMA((slots * ranks + group_heads,))],
        compiler_params=params,
        name="own",
    )(head_class, spatial, *back)
    merged = pl.pallas_call(
        functools.partial(merge_kernel, (group_heads, most, least)),
        out_shape=whole,
        in_specs=[smem, vmem, hbm],
        out_specs=hbm,
        scratch_shapes=[order, pltpu.SemaphoreType.DMA((handed,))],
        input_output_aliases={2: 0},
        compiler_params=params,
        name="merge",
    )(head_class, returned, mostly)
    return jnp.moveaxis(merged, 0, 1)[None]


def frame_attend(triple):
    query_block, key_block, value_block = triple
    scores = lax.dot_general(
        query_block, key_block, (((1,), (1,)), ((), ())), preferred_element_type=jnp.float32
    ) * (query_block.shape[-1] ** -0.5)
    exponent, totals = softmax_rows(scores)
    blended = jnp.dot(
        exponent.astype(jnp.bfloat16), value_block, preferred_element_type=jnp.float32
    )
    return (blended / totals).astype(jnp.bfloat16)


def run_spatial(triple):
    moved = tuple((jnp.moveaxis(a[0], 1, 0) for a in triple))
    blended = lax.map(frame_attend, moved)
    return jnp.moveaxis(blended, 0, 1)[None]


def run_temporal(triple, frame_mask):
    query_block, key_block, value_block = (
        lax.all_to_all(a, "tm", split_axis=1, concat_axis=0, tiled=True) for a in triple
    )
    score_scale = query_block.shape[-1] ** (-0.5)
    frame_total = query_block.shape[0]
    block_total = frame_mask.shape[0]
    frame_block = jnp.arange(frame_total, dtype=jnp.int32) // (frame_total // block_total)
    onehot = (frame_block[:, None] == jnp.arange(block_total, dtype=jnp.int32)[None, :]).astype(
        jnp.float32
    )
    allowed = jnp.dot(jnp.dot(onehot, frame_mask.astype(jnp.float32)), onehot.T) > 0.5
    scores = (
        jnp.einsum("fpmd,gpmd->pmfg", query_block, key_block, preferred_element_type=jnp.float32)
        * score_scale
    )
    scores = jnp.where(allowed, scores, jnp.float32(NEGATIVE))
    peak = jnp.max(scores, axis=-1, keepdims=True)
    exponent = jnp.where(allowed, jnp.exp(scores - peak), jnp.float32(0.0))
    totals = jnp.sum(exponent, axis=-1)
    blended = jnp.einsum(
        "pmfg,gpmd->fpmd",
        exponent.astype(jnp.bfloat16),
        value_block,
        preferred_element_type=jnp.float32,
    )
    result = (blended / jnp.transpose(totals, (2, 0, 1))[..., None]).astype(jnp.bfloat16)
    return lax.all_to_all(result, "tm", split_axis=0, concat_axis=1, tiled=True)


def per_device_many(queries, key_vectors, value_vectors, head_class, frame_mask):
    group_heads = queries.shape[2]
    moved_heads = group_heads // 3
    half_heads = group_heads // 2
    least_count = half_heads - moved_heads
    most_count = half_heads + moved_heads
    head_group = lax.axis_index("head")
    local_class = lax.dynamic_slice_in_dim(head_class, head_group * group_heads, group_heads)
    sorted_heads = jnp.argsort(local_class, stable=True)
    head_rank = jnp.argsort(sorted_heads)
    temporal_count = jnp.sum(local_class)
    position = jnp.arange(group_heads, dtype=jnp.int32)
    triple = (queries, key_vectors, value_vectors)
    spatial_in = tuple((jnp.take(a, sorted_heads[:most_count], axis=2) for a in triple))
    temporal_in = tuple((jnp.take(a, sorted_heads[least_count:], axis=2) for a in triple))
    spatial_out = run_spatial(spatial_in)
    temporal_out = run_temporal(temporal_in, frame_mask)
    result_pool = jnp.concatenate([spatial_out, temporal_out], axis=2)
    slot_index = jnp.where(
        position < group_heads - temporal_count, position, most_count + position - least_count
    )
    return jnp.take(result_pool, jnp.take(slot_index, head_rank), axis=2)


def solution(mesh):
    ranks, head_total = mesh.shape["tm"], mesh.shape["head"]
    spec = P("tm", None, "head", None)

    def whole(queries, key_vectors, value_vectors, head_class, frame_mask):
        few = (
            ranks & (ranks - 1) == 0
            and 2 <= ranks <= 8
            and queries.shape[0] == ranks
            and queries.shape[1] % (ranks * ROWS) == 0
            and head_total % 2 == 0
            and ranks % frame_mask.shape[0] == 0
        )
        body = functools.partial(per_device, head_total) if few else per_device_many
        return jax.shard_map(
            body, mesh=mesh, in_specs=(spec, spec, spec, P(), P()), out_specs=spec, check_vma=False
        )(queries, key_vectors, value_vectors, head_class, frame_mask)

    return whole
```
